256 devices in a mesh: batch: 32 (over x, y, core), tensor: 8 (over z).
Axes of the slice: x: 4, y: 4, z: 8, core: 2. Of those that a mesh axis runs over, the one named last changes fastest.
Arguments:
- residual: bfloat16 [256, 2, 4096], P('batch', None, 'tensor'), may hold values from -64 to 64
- new_queries: bfloat16 [256, 2, 2048], P('batch', None, 'tensor'), may hold values from -5 to 5
- new_keys: bfloat16 [256, 2, 2048], P('batch', None, 'tensor'), may hold values from -5 to 5
- new_values: bfloat16 [256, 2, 2048], P('batch', None, 'tensor'), may hold values from -5 to 5
- cache_keys: bfloat16 [256, 256, 2048], P('batch', None, 'tensor'), may hold values from -5 to 5
- cache_values: bfloat16 [256, 256, 2048], P('batch', None, 'tensor'), may hold values from -5 to 5
- lengths: int32 [256], P('batch'), may hold values from 2 to 256, as said below
- out_weight: bfloat16 [2048, 4096], P('tensor'), may hold values from -0.5 to 0.5
- temporal_gain: bfloat16 [4096], P('tensor'), may hold values from 0.099609375 to 1.8984375
- in_weight: bfloat16 [4096, 1024], P('tensor'), may hold values from -0.09375 to 0.09375
- tokens: int32 [256, 2, 8], P(('batch', 'tensor')), may hold values from 0 to 2047
- level_tables: bfloat16 [8, 2048, 1024], P(None, 'batch'), may hold values from -5 to 5
- depth_gain: bfloat16 [1024], replicated, may hold values from 0.099609375 to 1.8984375
- depth_qkv: bfloat16 [1024, 1536], replicated, may hold values from -0.1875 to 0.1875
- depth_out: bfloat16 [512, 1024], replicated, may hold values from -0.25 to 0.25
Outputs:
- temporal_out: bfloat16 [256, 2, 4096], P('batch', None, 'tensor')
- depth_states: bfloat16 [256, 2, 8, 1024], P(('batch', 'tensor'))
The draws below stay inside these ranges and needn't reach their ends.
Inputs may be any that keep to these rules, and one draw needn't show every extreme that they name: `lengths`: each dialogue has between 2 and 256 live cache slots, the first ones; in every draw some dialogue has exactly 256.
All inputs are finite; a program needn't handle non-finite values.
Results may differ from the reference program's by a relative error of at most 0.02.
Values may be sent and summed in bfloat16 or wider, within the bound.
No kernel may reach another device: no remote copies, remote signals or barrier semaphores. Data moves between devices by JAX's collectives and lax.ppermute only.
A program may use at most 64 MiB of HBM per device.

```python
import math
import jax
import jax.numpy as jnp
from jax import lax

D = 4096
HD = 128
HEADS = 16
DD = 1024
DHD = 64
DHEADS = 8
VOCAB = 2048
LEVELS = 8
FRAMES = 2
CACHE = 256
DLG_DEV = 8
QW = 2048
DH = 512
DIALOGUES = 256


def draw_new_queries(key, part):
    key = jax.random.fold_in(key, 1)
    base = jax.random.truncated_normal(key, -4.5, 4.5, (DIALOGUES, FRAMES, HEADS * HD), jnp.float32)
    return base.astype(jnp.bfloat16)


def draw_cache_keys(key, part):
    key = jax.random.fold_in(key, 2)
    base = jax.random.truncated_normal(key, -4.5, 4.5, (DIALOGUES, CACHE, HEADS * HD), jnp.float32)
    return base.astype(jnp.bfloat16)


def draw_residual(key, part):
    key = jax.random.fold_in(key, 3)
    key_base, key_row, key_col = jax.random.split(key, 3)
    row_scale = jnp.exp(jax.random.uniform(key_row, (DIALOGUES, FRAMES, 1), jnp.float32, math.log(0.3), math.log(3.0)))
    col_spread = jnp.exp(jax.random.uniform(key_col, (1, 1, D), jnp.float32, math.log(0.5), math.log(1.7)))
    placing = jnp.arange(D, dtype=jnp.float32)[None, None, :] / D
    base = jax.random.truncated_normal(key_base, -4.0, 4.0, (DIALOGUES, FRAMES, D), jnp.float32)
    col_scale = col_spread * jnp.exp(placing * math.log(3.0))
    return (base * row_scale * col_scale).astype(jnp.bfloat16)


def draw_lengths(key, part):
    key = jax.random.fold_in(key, 4)
    key_len, key_group, key_pick = jax.random.split(key, 3)
    raw_len = jax.random.randint(key_len, (DIALOGUES,), 0, CACHE - 1)
    factor = jax.random.randint(key_group, (DIALOGUES // DLG_DEV,), 1, 5)
    factor = jnp.repeat(factor, DLG_DEV, total_repeat_length=DIALOGUES)
    spans = 2 + raw_len * factor // 4
    picked = jax.random.randint(key_pick, (), 0, DIALOGUES)
    return jnp.where(jnp.arange(DIALOGUES) == picked, CACHE, spans).astype(jnp.int32)


def place_ends(drawn, rng, low, top_value):
    spot = [jax.random.randint(jax.random.fold_in(rng, axis), (), 0, length) for axis, length in enumerate(drawn.shape)]
    longest = drawn.shape.index(max(drawn.shape))
    beside = spot[:longest] + [(spot[longest] + 1) % drawn.shape[longest]] + spot[longest + 1:]
    return drawn.at[tuple(spot)].set(low).at[tuple(beside)].set(top_value)


def steps_of(own_key, extent, pieces, low, high):
    def one(axis_at, shards_of):
        draws = jax.random.uniform(jax.random.fold_in(jax.random.fold_in(own_key, 6), axis_at), (shards_of,), jnp.float32, low / len(pieces), high / len(pieces))
        return jnp.repeat(jnp.exp(draws), extent[axis_at] // shards_of).reshape((-1,) + (1,) * (len(extent) - axis_at - 1))

    gain = one(*pieces[0])
    for cut in pieces[1:]:
        gain = gain * one(*cut)
    return gain


def bell_draw(stream_key, shape, deviation, bound, shards=(), kind=jnp.bfloat16):
    entries = deviation * jax.random.normal(stream_key, shape, jnp.float32)
    if shards:
        entries = entries * steps_of(stream_key, shape, shards, -0.22, 0.18)
    return jnp.clip(entries, -bound, bound).astype(kind)


def setup_inputs(seed: int = 0) -> dict:
    streams_of = jax.random.split(jax.random.key(seed), 16)
    return {
        "residual": draw_residual(jax.random.fold_in(streams_of[15], 71), 0),
        "new_queries": draw_new_queries(jax.random.fold_in(streams_of[15], 71), 0),
        "new_keys": bell_draw(streams_of[2], (DIALOGUES, FRAMES, QW), 1.0, 5.0, ((0, 32), (2, 8))),
        "new_values": bell_draw(streams_of[3], (DIALOGUES, FRAMES, QW), 1.0, 5.0, ((0, 32), (2, 8))),
        "cache_keys": draw_cache_keys(jax.random.fold_in(streams_of[15], 71), 0),
        "cache_values": bell_draw(streams_of[5], (DIALOGUES, CACHE, QW), 1.0, 5.0, ((0, 32), (2, 8))),
        "lengths": draw_lengths(jax.random.fold_in(streams_of[15], 71), 0),
        "out_weight": bell_draw(streams_of[7], (QW, D), HD ** -0.5, 0.5, ((0, 8),)),
        "temporal_gain": jnp.clip(1.0 + 0.18 * jax.random.normal(streams_of[8], (D,), jnp.float32), 0.099609375, 1.8984375).astype(jnp.bfloat16),
        "in_weight": bell_draw(streams_of[9], (D, DD), D ** -0.5, 0.09375, ((0, 8),)),
        "tokens": place_ends(jax.random.randint(streams_of[10], (DIALOGUES, FRAMES, LEVELS), 0, VOCAB), jax.random.fold_in(streams_of[10], 1), 0, VOCAB - 1).astype(jnp.int32),
        "level_tables": bell_draw(streams_of[11], (LEVELS, VOCAB, DD), 1.0, 5.0, ((1, 32),)),
        "depth_gain": jnp.clip(1.0 + 0.18 * jax.random.normal(streams_of[12], (DD,), jnp.float32), 0.099609375, 1.8984375).astype(jnp.bfloat16),
        "depth_qkv": bell_draw(streams_of[13], (DD, 3 * DH), DD ** -0.5, 0.1875),
        "depth_out": bell_draw(streams_of[14], (DH, DD), DH ** -0.5, 0.25),
    }


def inverse_rms(values, count):
    return lax.rsqrt(lax.optimization_barrier(jnp.sum(values * values, axis=-1, keepdims=True)) / count + 1e-05)

def reference(residual, new_queries, new_keys, new_values, cache_keys, cache_values, lengths, out_weight, temporal_gain, in_weight, tokens, level_tables, depth_gain, depth_qkv, depth_out):
    dialogues = residual.shape[0]
    score_scale = 1.0 / math.sqrt(HD)
    queries = new_queries.reshape(dialogues, FRAMES, HEADS, HD).astype(jnp.float32)
    fresh_keys = new_keys.reshape(dialogues, FRAMES, HEADS, HD).astype(jnp.float32)
    fresh_values = new_values.reshape(dialogues, FRAMES, HEADS, HD).astype(jnp.float32)
    past_keys = cache_keys.reshape(dialogues, CACHE, HEADS, HD).astype(jnp.float32)
    past_values = cache_values.reshape(dialogues, CACHE, HEADS, HD).astype(jnp.float32)
    live_slots = (jnp.arange(CACHE, dtype=jnp.int32)[None, :] < lengths[:, None])[:, None, None, :]
    frame_mask = jnp.arange(FRAMES)[:, None] >= jnp.arange(FRAMES)[None, :]
    score_cache = jnp.einsum('dfhe,dche->dhfc', queries, past_keys) * score_scale
    score_cache = jnp.where(live_slots, score_cache, -jnp.inf)
    score_fresh = jnp.einsum('dfhe,dghe->dhfg', queries, fresh_keys) * score_scale
    score_fresh = jnp.where(frame_mask[None, None], score_fresh, -jnp.inf)
    largest = jnp.maximum(lax.optimization_barrier(jnp.max(score_cache, axis=-1, keepdims=True)), lax.optimization_barrier(jnp.max(score_fresh, axis=-1, keepdims=True)))
    exp_cache = jnp.exp(score_cache - largest)
    exp_fresh = jnp.exp(score_fresh - largest)
    total = lax.optimization_barrier(jnp.sum(exp_cache, axis=-1, keepdims=True)) + lax.optimization_barrier(jnp.sum(exp_fresh, axis=-1, keepdims=True))
    prob_cache = (exp_cache / total).astype(jnp.bfloat16).astype(jnp.float32)
    prob_fresh = (exp_fresh / total).astype(jnp.bfloat16).astype(jnp.float32)
    attended = jnp.einsum('dhfc,dche->dfhe', prob_cache, past_values) + jnp.einsum('dhfg,dghe->dfhe', prob_fresh, fresh_values)
    attended = attended.reshape(dialogues * FRAMES, QW).astype(jnp.bfloat16)
    stream = residual.astype(jnp.float32) + jnp.dot(attended, out_weight, preferred_element_type=jnp.float32).reshape(dialogues, FRAMES, D)
    temporal_out = stream.astype(jnp.bfloat16)
    normed = (stream * inverse_rms(stream, D) * temporal_gain.astype(jnp.float32)).astype(jnp.bfloat16)
    depth_proj = jnp.dot(normed.reshape(dialogues * FRAMES, D), in_weight, preferred_element_type=jnp.float32).reshape(dialogues, FRAMES, 1, DD)
    level_index = jnp.arange(LEVELS, dtype=jnp.int32)[None, None, :]
    table_rows = level_tables[level_index, tokens].astype(jnp.float32)
    depth_input = depth_proj + table_rows
    depth_normed = (depth_input * inverse_rms(depth_input, DD) * depth_gain.astype(jnp.float32)).astype(jnp.bfloat16)
    projected = jnp.dot(depth_normed.reshape(-1, DD), depth_qkv, preferred_element_type=jnp.float32).astype(jnp.bfloat16)
    projected = projected.reshape(dialogues, FRAMES, LEVELS, 3, DHEADS, DHD).astype(jnp.float32)
    depth_query = projected[:, :, :, 0]
    depth_key = projected[:, :, :, 1]
    depth_value = projected[:, :, :, 2]
    depth_scores = jnp.einsum('aflhe,afmhe->afhlm', depth_query, depth_key) / math.sqrt(DHD)
    causal_mask = jnp.arange(LEVELS)[:, None] >= jnp.arange(LEVELS)[None, :]
    depth_exp = jnp.where(causal_mask, jnp.exp(depth_scores), 0.0)
    depth_probs = (depth_exp / lax.optimization_barrier(jnp.sum(depth_exp, axis=-1, keepdims=True))).astype(jnp.bfloat16).astype(jnp.float32)
    depth_mixed = jnp.einsum('afhlm,afmhe->aflhe', depth_probs, depth_value).astype(jnp.bfloat16).reshape(-1, DH)
    depth_states = depth_input + jnp.dot(depth_mixed, depth_out, preferred_element_type=jnp.float32).reshape(dialogues, FRAMES, LEVELS, DD)
    return (temporal_out, depth_states.astype(jnp.bfloat16))
```

```python
import math

import jax
import jax.numpy as jnp
from jax import lax
from jax.sharding import PartitionSpec as P

D = 4096
HD = 128
DHD = 64
DHEADS = 8
LEVELS = 8
FRAMES = 2


def inverse_rms(values, count):
    return lax.rsqrt(jnp.sum(values * values, axis=-1, keepdims=True) / count + 1e-05)


def per_device(
    residual,
    new_queries,
    new_keys,
    new_values,
    cache_keys,
    cache_values,
    lengths,
    out_weight,
    temporal_gain,
    in_weight,
    tokens,
    level_tables,
    depth_gain,
    depth_qkv,
    depth_out,
):
    held_dialogues = residual.shape[0]
    features = residual.shape[2]
    head_width = new_queries.shape[2]
    head_count = head_width // HD
    cache_len = cache_keys.shape[1]
    score_scale = 1.0 / math.sqrt(HD)
    queries = new_queries.reshape(held_dialogues, FRAMES, head_count, HD)
    fresh_keys = new_keys.reshape(held_dialogues, FRAMES, head_count, HD)
    fresh_values = new_values.reshape(held_dialogues, FRAMES, head_count, HD)
    past_keys = cache_keys.reshape(held_dialogues, cache_len, head_count, HD)
    past_values = cache_values.reshape(held_dialogues, cache_len, head_count, HD)
    live_slots = (jnp.arange(cache_len, dtype=jnp.int32)[None, :] < lengths[:, None])[
        :, None, None, :
    ]
    frame_mask = jnp.arange(FRAMES)[:, None] >= jnp.arange(FRAMES)[None, :]
    score_cache = (
        jnp.einsum("dfhe,dche->dhfc", queries, past_keys, preferred_element_type=jnp.float32)
        * score_scale
    )
    score_cache = jnp.where(live_slots, score_cache, -jnp.inf)
    score_fresh = (
        jnp.einsum("dfhe,dghe->dhfg", queries, fresh_keys, preferred_element_type=jnp.float32)
        * score_scale
    )
    score_fresh = jnp.where(frame_mask[None, None], score_fresh, -jnp.inf)
    largest = jnp.maximum(
        jnp.max(score_cache, axis=-1, keepdims=True), jnp.max(score_fresh, axis=-1, keepdims=True)
    )
    exp_cache = jnp.exp(score_cache - largest)
    exp_fresh = jnp.exp(score_fresh - largest)
    total = jnp.sum(exp_cache, axis=-1, keepdims=True) + jnp.sum(exp_fresh, axis=-1, keepdims=True)
    prob_cache = (exp_cache / total).astype(jnp.bfloat16)
    prob_fresh = (exp_fresh / total).astype(jnp.bfloat16)
    attended = jnp.einsum(
        "dhfc,dche->dfhe", prob_cache, past_values, preferred_element_type=jnp.float32
    )
    attended = attended + jnp.einsum(
        "dhfg,dghe->dfhe", prob_fresh, fresh_values, preferred_element_type=jnp.float32
    )
    attended = attended.astype(jnp.bfloat16).reshape(held_dialogues * FRAMES, head_width)
    tensor_size = lax.axis_size("tensor")
    batch_size = lax.axis_size("batch")
    rows = held_dialogues * FRAMES
    owned_dialogues = held_dialogues // tensor_size

    token_count = owned_dialogues * FRAMES * LEVELS
    sent_ids = jnp.broadcast_to(tokens.reshape(1, token_count), (batch_size, token_count))
    gathered_ids = lax.all_to_all(sent_ids, "batch", 0, 0, tiled=True)
    vocab_span = level_tables.shape[1]
    vocab_start = lax.axis_index("batch") * vocab_span
    levels = jnp.arange(token_count, dtype=jnp.int32) % LEVELS
    local_ids = gathered_ids - vocab_start
    entry = jnp.where(
        (local_ids >= 0) & (local_ids < vocab_span), local_ids + levels * vocab_span, -1
    ).reshape(-1, 1)
    one_hot = (entry == jnp.arange(LEVELS * vocab_span, dtype=jnp.int32)[None, :]).astype(
        jnp.bfloat16
    )
    partial_rows = jnp.dot(
        one_hot,
        level_tables.reshape(LEVELS * vocab_span, -1),
        preferred_element_type=jnp.float32,
    ).astype(jnp.bfloat16)
    received_rows = lax.all_to_all(
        partial_rows.reshape(batch_size, token_count, -1), "batch", 0, 0, tiled=True
    )
    table_rows = jnp.sum(received_rows.astype(jnp.float32), axis=0)

    head_terms = jnp.dot(attended, out_weight, preferred_element_type=jnp.float32)
    head_terms = head_terms.astype(jnp.bfloat16).reshape(rows, tensor_size, features)
    head_terms = head_terms.transpose(1, 0, 2)
    shares = lax.all_to_all(head_terms, "tensor", 0, 0, tiled=True)
    shares = jnp.sum(shares.astype(jnp.float32), axis=0)
    hidden = residual.astype(jnp.float32).reshape(rows, features) + shares
    temporal_out = hidden.astype(jnp.bfloat16).reshape(held_dialogues, FRAMES, features)
    squares = jnp.sum(hidden * hidden, axis=-1, keepdims=True)
    scaled = (hidden * temporal_gain.astype(jnp.float32)).astype(jnp.bfloat16)
    product = jnp.dot(scaled, in_weight, preferred_element_type=jnp.float32)
    payload = jnp.concatenate([product, jnp.broadcast_to(squares, (rows, 128))], axis=1)
    payload = payload.reshape(tensor_size, owned_dialogues * FRAMES, -1)
    received = lax.all_to_all(payload, "tensor", 0, 0, tiled=True)
    received = jnp.sum(received, axis=0)
    depth_proj = received[:, :-128]
    inverse = lax.rsqrt(received[:, -128:-127] / D + 1e-05)
    depth_proj = (depth_proj * inverse).reshape(owned_dialogues, FRAMES, -1)
    depth_input = depth_proj[:, :, None, :] + table_rows.reshape(
        owned_dialogues, FRAMES, LEVELS, -1
    )
    depth_width = depth_input.shape[3]
    depth_normed = (
        depth_input * inverse_rms(depth_input, depth_width) * depth_gain.astype(jnp.float32)
    ).astype(jnp.bfloat16)
    projected = jnp.dot(
        depth_normed.reshape(-1, depth_width), depth_qkv, preferred_element_type=jnp.float32
    ).astype(jnp.bfloat16)
    projected = projected.reshape(owned_dialogues, FRAMES, LEVELS, 3, DHEADS, DHD)
    depth_query = projected[:, :, :, 0]
    depth_key = projected[:, :, :, 1]
    depth_value = projected[:, :, :, 2]
    depth_scores = jnp.einsum(
        "aflhe,afmhe->afhlm", depth_query, depth_key, preferred_element_type=jnp.float32
    ) / math.sqrt(DHD)
    causal_mask = jnp.arange(LEVELS)[:, None] >= jnp.arange(LEVELS)[None, :]
    depth_exp = jnp.where(causal_mask, jnp.exp(depth_scores), 0.0)
    depth_probs = (depth_exp / jnp.sum(depth_exp, axis=-1, keepdims=True)).astype(jnp.bfloat16)
    depth_mixed = jnp.einsum(
        "afhlm,afmhe->aflhe", depth_probs, depth_value, preferred_element_type=jnp.float32
    )
    depth_mixed = depth_mixed.astype(jnp.bfloat16).reshape(-1, DHEADS * DHD)
    depth_states = depth_input + jnp.dot(
        depth_mixed, depth_out, preferred_element_type=jnp.float32
    ).reshape(owned_dialogues, FRAMES, LEVELS, depth_width)
    return (temporal_out, depth_states.astype(jnp.bfloat16))


def solution(mesh):
    placed = (
        P("batch", None, "tensor"),
        P("batch", None, "tensor"),
        P("batch", None, "tensor"),
        P("batch", None, "tensor"),
        P("batch", None, "tensor"),
        P("batch", None, "tensor"),
        P("batch"),
        P("tensor", None),
        P("tensor"),
        P("tensor", None),
        P(("batch", "tensor"), None, None),
        P(None, "batch", None),
        P(),
        P(),
        P(),
    )
    return jax.shard_map(
        per_device,
        mesh=mesh,
        in_specs=placed,
        out_specs=(P("batch", None, "tensor"), P(("batch", "tensor"), None, None, None)),
        check_vma=False,
    )
```

```python
import functools
import math

import jax
import jax.numpy as jnp
from jax import lax
from jax.experimental import pallas as pl
from jax.experimental.pallas import tpu as pltpu
from jax.sharding import PartitionSpec as P

D = 4096
HD = 128
DD = 1024
DHD = 64
DHEADS = 8
LEVELS = 8
FRAMES = 2
CORES = 2
SIDE = 4
EXTRA = 128
MIB = 2**20
NT = (((1,), (1,)), ((), ()))


def dot_nt(a, b):
    return lax.dot_general(a, b, NT, preferred_element_type=jnp.float32)


def dot_nn(a, b):
    return jnp.dot(a, b, preferred_element_type=jnp.float32)


def iota(shape, axis):
    return lax.broadcasted_iota(jnp.int32, shape, axis)


def attend_kernel(
    lengths_ref, q_ref, nk_ref, nv_ref, k_hbm, v_hbm, w_hbm, out_ref, k_buf, v_buf, w_buf, small, sems
):
    dialogues = q_ref.shape[0]
    width = q_ref.shape[2]
    rows = dialogues * FRAMES
    heads = width // HD
    stacked = heads * rows
    half = dialogues // 2
    slots = k_buf.shape[1]
    copies = []
    for i in range(2):
        part = pl.ds(i * half, half)
        copies.append(pltpu.make_async_copy(k_hbm.at[part], k_buf.at[part], sems.at[i]))
    for i in range(2):
        part = pl.ds(i * half, half)
        copies.append(pltpu.make_async_copy(v_hbm.at[part], v_buf.at[part], sems.at[2 + i]))
    copies.append(pltpu.make_async_copy(w_hbm, w_buf, sems.at[4]))
    for copy in copies:
        copy.start()
    for i, ref in enumerate((q_ref, nk_ref, nv_ref)):
        for d in range(dialogues):
            small[i, FRAMES * d : FRAMES * (d + 1), :] = ref[d].astype(jnp.float32)
    query = small[0]
    fresh_key = small[1].astype(jnp.bfloat16)
    fresh_value = small[2].astype(jnp.bfloat16)
    head_of = iota((rows, width), 1) // HD
    spread = jnp.concatenate(
        [jnp.where(head_of == h, query, 0.0) for h in range(heads)], axis=0
    ).astype(jnp.bfloat16)
    scale = 1.0 / math.sqrt(HD)

    row = iota((stacked, slots), 0)
    slot = iota((stacked, slots), 1)
    dialogue = (row % rows) // FRAMES
    scores = jnp.zeros((stacked, slots), jnp.float32)
    live = jnp.zeros((stacked, slots), jnp.int32)
    for d in range(dialogues):
        if d % half == 0:
            copies[d // half].wait()
        scores = jnp.where(dialogue == d, dot_nt(spread, k_buf[d]), scores)
        live = jnp.where(dialogue == d, lengths_ref[d], live)
    scores = jnp.where(slot < live, scores * scale, -jnp.inf)

    row_n = iota((stacked, rows), 0) % rows
    col_n = iota((stacked, rows), 1)
    seen = (row_n // FRAMES == col_n // FRAMES) & (col_n <= row_n)
    fresh = jnp.where(seen, dot_nt(spread, fresh_key) * scale, -jnp.inf)
    largest = jnp.maximum(
        jnp.max(scores, axis=-1, keepdims=True), jnp.max(fresh, axis=-1, keepdims=True)
    )
    exp_cache = jnp.exp(scores - largest)
    exp_fresh = jnp.exp(fresh - largest)
    total = jnp.sum(exp_cache, axis=-1, keepdims=True) + jnp.sum(
        exp_fresh, axis=-1, keepdims=True
    )
    prob_cache = exp_cache / total
    prob_fresh = (exp_fresh / total).astype(jnp.bfloat16)
    mixed = dot_nn(prob_fresh, fresh_value)
    for d in range(dialogues):
        if d % half == 0:
            copies[2 + d // half].wait()
        own = jnp.where(dialogue == d, prob_cache, 0.0).astype(jnp.bfloat16)
        mixed = mixed + dot_nn(own, v_buf[d])
    attended = mixed[:rows]
    for h in range(1, heads):
        attended = jnp.where(head_of == h, mixed[h * rows : (h + 1) * rows], attended)
    attended = attended.astype(jnp.bfloat16)
    copies[4].wait()
    peers, _, features = out_ref.shape
    for t in range(peers):
        out_ref[t] = dot_nn(attended, w_buf[:, t * features : (t + 1) * features]).astype(
            jnp.bfloat16
        )


def lookup_kernel(ids_ref, own_hbm, other_ref, *refs):
    out_refs, (done_ref, own_buf, found_buf, sem) = refs[:SIDE], refs[SIDE:]
    first = pltpu.make_async_copy(own_hbm, own_buf, sem)
    first.start()
    members = ids_ref.shape[0]
    span = own_buf.shape[1]
    width = own_buf.shape[2]
    entries = LEVELS * span
    count = FRAMES * LEVELS
    rows = members * count
    me = lax.axis_index("batch")

    pick = (iota((rows, members), 0) // count == iota((rows, members), 1)).astype(jnp.bfloat16)
    row = iota((rows, LEVELS), 0)
    lane = iota((rows, LEVELS), 1)
    block = jnp.zeros((rows, LEVELS), jnp.float32)
    inner = jnp.zeros((rows, LEVELS), jnp.float32)
    for f in range(FRAMES):
        ids = ids_ref[:, f, :]
        mine = (lane == row % LEVELS) & ((row // LEVELS) % FRAMES == f)
        high = (ids // span).astype(jnp.float32).astype(jnp.bfloat16)
        low = (ids % span).astype(jnp.float32).astype(jnp.bfloat16)
        block = jnp.where(mine, dot_nn(pick, high), block)
        inner = jnp.where(mine, dot_nn(pick, low), inner)
    block = jnp.sum(block, axis=1, keepdims=True).astype(jnp.int32)
    inner = jnp.sum(inner, axis=1, keepdims=True).astype(jnp.int32)
    level = iota((rows, 1), 0) % LEVELS
    place = inner + level * span
    at_own = jnp.where(block == me, place, -1)
    at_other = jnp.where(block == (me ^ 1), place, -1)
    entry = iota((rows, entries), 1)
    hot_own = jnp.where(entry == at_own, 1.0, 0.0).astype(jnp.bfloat16)
    hot_other = jnp.where(entry == at_other, 1.0, 0.0).astype(jnp.bfloat16)
    first.wait()
    found = dot_nn(hot_own, own_buf[...].reshape(entries, width))
    found = found + dot_nn(hot_other, other_ref[...].reshape(entries, width))
    found_buf[...] = found.astype(jnp.bfloat16).reshape(found_buf.shape)
    mine = me // (SIDE * CORES)
    for s in range(SIDE):
        out_refs[s][...] = found_buf[pl.ds((mine + s) % SIDE * SIDE, SIDE)]
    done_ref[...] = jnp.zeros_like(done_ref)


def collect_kernel(own_ref, *refs):
    arrived, out_refs = refs[: SIDE - 1], refs[SIDE - 1 :]
    mine = lax.axis_index("batch") // CORES % SIDE
    for s in range(SIDE):
        place = (mine + s) % SIDE
        value = own_ref[place]
        for ref in arrived:
            value = value + ref[place]
        out_refs[s][...] = value


def middle_kernel(
    shares_ref, residual_ref, gain_ref, w_hbm, order_hbm, stream_ref, sent_ref, w_buf, rows_buf, sent_buf, sem
):
    copy = pltpu.make_async_copy(w_hbm, w_buf, sem)
    copy.start()
    dialogues = residual_ref.shape[0]
    for d in range(dialogues):
        rows_buf[FRAMES * d : FRAMES * (d + 1), :] = residual_ref[d].astype(jnp.float32)
    hidden = rows_buf[...]
    share = shares_ref[0].astype(jnp.float32)
    for t in range(1, shares_ref.shape[0]):
        share = share + shares_ref[t].astype(jnp.float32)
    hidden = hidden + share
    rows_buf[...] = hidden
    squares = jnp.sum(hidden * hidden, axis=-1, keepdims=True)
    scaled = (hidden * gain_ref[...]).astype(jnp.bfloat16)
    width = w_buf.shape[1]
    sent_buf[:, width:] = jnp.broadcast_to(squares, (hidden.shape[0], EXTRA))
    for d in range(dialogues):
        stream_ref[d] = rows_buf[FRAMES * d : FRAMES * (d + 1), :].astype(jnp.bfloat16)
    copy.wait()
    sent_buf[:, :width] = dot_nn(scaled, w_buf[...])
    for d in range(dialogues):
        sent_ref[d] = sent_buf[FRAMES * d : FRAMES * (d + 1), :]


def depth_kernel(
    terms_ref, *refs
):
    table_refs = refs[:SIDE]
    gain_ref, qkv_hbm, o_hbm, out_ref, qkv_buf, o_buf, sems = refs[SIDE:]
    first = pltpu.make_async_copy(qkv_hbm, qkv_buf, sems.at[0])
    second = pltpu.make_async_copy(o_hbm, o_buf, sems.at[1])
    first.start()
    second.start()
    count, width = table_refs[0].shape
    terms = terms_ref[0]
    for t in range(1, terms_ref.shape[0]):
        terms = terms + terms_ref[t]
    inverse = lax.rsqrt(terms[:, width : width + 1] / D + 1e-05)
    proj = terms[:, :width] * inverse
    values = table_refs[0][...].astype(jnp.float32)
    for ref in table_refs[1:]:
        values = values + ref[...].astype(jnp.float32)
    frame = iota((count, width), 0) // LEVELS
    depth_input = values + jnp.where(frame == 0, proj[0:1], proj[1:2])
    mean = jnp.sum(depth_input * depth_input, axis=-1, keepdims=True) / width
    normed = (depth_input * lax.rsqrt(mean + 1e-05) * gain_ref[...]).astype(jnp.bfloat16)
    first.wait()
    heads_width = DHEADS * DHD
    query = dot_nn(normed, qkv_buf[:, :heads_width]).astype(jnp.bfloat16).astype(jnp.float32)
    key = dot_nn(normed, qkv_buf[:, heads_width : 2 * heads_width]).astype(jnp.bfloat16)
    value = dot_nn(normed, qkv_buf[:, 2 * heads_width :]).astype(jnp.bfloat16)
    head_of = iota((count, heads_width), 1) // DHD
    spread = jnp.concatenate(
        [jnp.where(head_of == h, query, 0.0) for h in range(DHEADS)], axis=0
    ).astype(jnp.bfloat16)
    scores = dot_nt(spread, key) * (1.0 / math.sqrt(DHD))
    row = iota(scores.shape, 0) % count
    col = iota(scores.shape, 1)
    seen = (row // LEVELS == col // LEVELS) & (col <= row)
    exps = jnp.where(seen, jnp.exp(scores), 0.0)
    probs = (exps / jnp.sum(exps, axis=-1, keepdims=True)).astype(jnp.bfloat16)
    spread_out = dot_nn(probs, value)
    mixed = spread_out[:count]
    for h in range(1, DHEADS):
        mixed = jnp.where(head_of == h, spread_out[h * count : (h + 1) * count], mixed)
    second.wait()
    out_ref[...] = (depth_input + dot_nn(mixed.astype(jnp.bfloat16), o_buf[...])).astype(
        jnp.bfloat16
    )


VMEM = pl.BlockSpec(memory_space=pltpu.VMEM)
SMEM = pl.BlockSpec(memory_space=pltpu.SMEM)
ANY = pl.BlockSpec(memory_space=pl.ANY)


def hbm(*arrays):
    return tuple(pltpu.with_memory_space_constraint(a, pltpu.HBM) for a in arrays)


def call(kernel, name, outs, ins, out_specs, scratch, limit, flops, moved):
    return pl.pallas_call(
        kernel,
        name=name,
        out_shape=outs,
        in_specs=ins,
        out_specs=out_specs,
        scratch_shapes=scratch,
        compiler_params=pltpu.CompilerParams(vmem_limit_bytes=limit * MIB),
        cost_estimate=pl.CostEstimate(flops=flops, bytes_accessed=moved, transcendentals=0),
    )


def shifted(size, step, s):
    span = SIDE * step
    return [(b, b // span * span + (b + s * step) % span) for b in range(size)]


def per_device(
    residual,
    new_queries,
    new_keys,
    new_values,
    cache_keys,
    cache_values,
    lengths,
    out_weight,
    temporal_gain,
    in_weight,
    tokens,
    level_tables,
    depth_gain,
    depth_qkv,
    depth_out,
):
    shape = jax.ShapeDtypeStruct
    bf16, f32 = jnp.bfloat16, jnp.float32
    held, _, features = residual.shape
    tensor_size = lax.axis_size("tensor")
    batch_size = lax.axis_size("batch")
    rows = held * FRAMES
    width = in_weight.shape[1]
    members = batch_size // CORES
    groups = [[b for b in range(batch_size) if b % CORES == c] for c in range(CORES)]
    count = FRAMES * LEVELS

    other_tables = lax.ppermute(level_tables, "batch", [(b, b ^ 1) for b in range(batch_size)])
    sent_ids = jnp.broadcast_to(tokens, (members, FRAMES, LEVELS))
    ids = lax.all_to_all(sent_ids, "batch", 0, 0, axis_index_groups=groups, tiled=True)

    head_terms = call(
        attend_kernel,
        "attend",
        pltpu.HBM((tensor_size, rows, features), bf16),
        [SMEM, VMEM, VMEM, VMEM, ANY, ANY, ANY],
        VMEM,
        [
            pltpu.VMEM(cache_keys.shape, bf16),
            pltpu.VMEM(cache_values.shape, bf16),
            pltpu.VMEM(out_weight.shape, bf16),
            pltpu.VMEM((3, rows, new_queries.shape[2]), f32),
            pltpu.SemaphoreType.DMA((5,)),
        ],
        24,
        10**8,
        4 * 2**20,
    )(*hbm(lengths, new_queries, new_keys, new_values, cache_keys, cache_values, out_weight))
    shares = lax.all_to_all(head_terms, "tensor", 0, 0, tiled=True)

    *partial_rows, order = call(
        lookup_kernel,
        "lookup",
        (*[shape((SIDE, count, width), bf16)] * SIDE, shape((8, 128), f32)),
        [VMEM, ANY, VMEM],
        (*[VMEM] * SIDE, VMEM),
        [
            pltpu.VMEM(level_tables.shape, bf16),
            pltpu.VMEM((members, count, width), bf16),
            pltpu.SemaphoreType.DMA,
        ],
        24,
        6 * 10**8,
        1,
    )(ids, *hbm(level_tables), other_tables)
    across = [
        lax.ppermute(partial_rows[s], "batch", shifted(batch_size, SIDE * CORES, s))
        for s in (2, 1, 3)
    ]
    own_rows, *side_rows = call(
        collect_kernel,
        "collect",
        [shape((count, width), bf16)] * SIDE,
        [VMEM] * SIDE,
        [VMEM] * SIDE,
        [],
        24,
        10**6,
        1,
    )(partial_rows[0], *across)
    along = [
        lax.ppermute(side_rows[s - 1], "batch", shifted(batch_size, CORES, s)) for s in (2, 1, 3)
    ]

    temporal_out, sent = call(
        middle_kernel,
        "middle",
        (pltpu.HBM(residual.shape, bf16), pltpu.HBM((held, FRAMES, width + EXTRA), f32)),
        [VMEM, VMEM, VMEM, ANY, ANY],
        (VMEM, VMEM),
        [
            pltpu.VMEM(in_weight.shape, bf16),
            pltpu.VMEM((rows, features), f32),
            pltpu.VMEM((rows, width + EXTRA), f32),
            pltpu.SemaphoreType.DMA,
        ],
        24,
        10**9,
        1,
    )(shares, residual, temporal_gain.astype(f32).reshape(1, features), *hbm(in_weight), order)
    terms = lax.all_to_all(sent, "tensor", 0, 0, tiled=True)

    states = call(
        depth_kernel,
        "depth",
        pltpu.HBM((count, width), bf16),
        [VMEM] * (SIDE + 2) + [ANY, ANY],
        VMEM,
        [
            pltpu.VMEM(depth_qkv.shape, bf16),
            pltpu.VMEM(depth_out.shape, bf16),
            pltpu.SemaphoreType.DMA((2,)),
        ],
        24,
        10**9,
        1,
    )(terms, own_rows, *along, depth_gain.astype(f32).reshape(1, width), *hbm(depth_qkv, depth_out))
    return (temporal_out, states.reshape(1, FRAMES, LEVELS, width))


def solution(mesh):
    placed = (
        P("batch", None, "tensor"),
        P("batch", None, "tensor"),
        P("batch", None, "tensor"),
        P("batch", None, "tensor"),
        P("batch", None, "tensor"),
        P("batch", None, "tensor"),
        P("batch"),
        P("tensor", None),
        P("tensor"),
        P("tensor", None),
        P(("batch", "tensor"), None, None),
        P(None, "batch", None),
        P(),
        P(),
        P(),
    )
    return jax.shard_map(
        per_device,
        mesh=mesh,
        in_specs=placed,
        out_specs=(P("batch", None, "tensor"), P(("batch", "tensor"), None, None, None)),
        check_vma=False,
    )
```

```python
import functools
import math

import jax
import jax.numpy as jnp
from jax import lax
from jax.experimental import pallas as pl
from jax.experimental.pallas import tpu as pltpu
from jax.sharding import PartitionSpec as P

D = 4096
HD = 128
DD = 1024
DHD = 64
DHEADS = 8
LEVELS = 8
FRAMES = 2
CORES = 2
SIDE = 4
STEPS = (2, 1, 3)
EXTRA = 128
MIB = 2**20
LIMIT = 16
WARM_FLOPS = 10**10
NT = (((1,), (1,)), ((), ()))


def dot_nt(a, b):
    return lax.dot_general(a, b, NT, preferred_element_type=jnp.float32)


def dot_nn(a, b):
    return jnp.dot(a, b, preferred_element_type=jnp.float32)


def iota(shape, axis):
    return lax.broadcasted_iota(jnp.int32, shape, axis)


def warm_kernel(out_ref):
    out_ref[...] = jnp.zeros_like(out_ref)


def attend_kernel(
    lengths_hbm, q_ref, nk_ref, nv_ref, k_ref, v_hbm, w_ref, own_hbm, order_ref, out_hbm, own_ref,
    lengths_buf, v_buf, small, sent_buf, sems
):
    get_lengths = pltpu.make_async_copy(lengths_hbm, lengths_buf, sems.at[0])
    get_values = pltpu.make_async_copy(v_hbm, v_buf, sems.at[1])
    get_own = pltpu.make_async_copy(own_hbm, own_ref, sems.at[2])
    get_lengths.start()
    get_values.start()
    get_own.start()
    dialogues = q_ref.shape[0]
    width = q_ref.shape[2]
    rows = dialogues * FRAMES
    heads = width // HD
    stacked = heads * rows
    slots = k_ref.shape[1]
    for i, ref in enumerate((q_ref, nk_ref, nv_ref)):
        for d in range(dialogues):
            small[i, FRAMES * d : FRAMES * (d + 1), :] = ref[d].astype(jnp.float32)
    query = small[0]
    fresh_key = small[1].astype(jnp.bfloat16)
    fresh_value = small[2].astype(jnp.bfloat16)
    head_of = iota((rows, width), 1) // HD
    spread = jnp.concatenate(
        [jnp.where(head_of == h, query, 0.0) for h in range(heads)], axis=0
    ).astype(jnp.bfloat16)
    scale = 1.0 / math.sqrt(HD)

    row = iota((stacked, slots), 0)
    slot = iota((stacked, slots), 1)
    dialogue = (row % rows) // FRAMES
    scores = jnp.zeros((stacked, slots), jnp.float32)
    for d in range(dialogues):
        scores = jnp.where(dialogue == d, dot_nt(spread, k_ref[d]), scores)
    row_n = iota((stacked, rows), 0) % rows
    col_n = iota((stacked, rows), 1)
    seen = (row_n // FRAMES == col_n // FRAMES) & (col_n <= row_n)
    fresh = jnp.where(seen, dot_nt(spread, fresh_key) * scale, -jnp.inf)
    get_lengths.wait()
    live = jnp.zeros((stacked, slots), jnp.int32)
    for d in range(dialogues):
        live = jnp.where(dialogue == d, lengths_buf[d], live)
    scores = jnp.where(slot < live, scores * scale, -jnp.inf)
    largest = jnp.maximum(
        jnp.max(scores, axis=-1, keepdims=True), jnp.max(fresh, axis=-1, keepdims=True)
    )
    exp_cache = jnp.exp(scores - largest)
    exp_fresh = jnp.exp(fresh - largest)
    total = jnp.sum(exp_cache, axis=-1, keepdims=True) + jnp.sum(
        exp_fresh, axis=-1, keepdims=True
    )
    prob_cache = exp_cache / total
    prob_fresh = (exp_fresh / total).astype(jnp.bfloat16)
    mixed = dot_nn(prob_fresh, fresh_value)
    get_values.wait()
    for d in range(dialogues):
        own = jnp.where(dialogue == d, prob_cache, 0.0).astype(jnp.bfloat16)
        mixed = mixed + dot_nn(own, v_buf[d])
    attended = mixed[:rows]
    for h in range(1, heads):
        attended = jnp.where(head_of == h, mixed[h * rows : (h + 1) * rows], attended)
    attended = attended.astype(jnp.bfloat16)
    peers, _, features = sent_buf.shape
    sends = []
    for t in range(peers):
        sent_buf[t] = dot_nn(attended, w_ref[:, t * features : (t + 1) * features]).astype(
            jnp.bfloat16
        )
        sends.append(pltpu.make_async_copy(sent_buf.at[t], out_hbm.at[t], sems.at[3 + t]))
        sends[t].start()
    get_own.wait()
    for send in sends:
        send.wait()


def gather_kernel(*refs):
    out_ref = refs[-1]
    for i in range(SIDE):
        out_ref[i] = refs[i][0]


def lookup_kernel(*refs):
    ids_refs, (own_ref, other_ref) = refs[:SIDE], refs[SIDE : SIDE + 2]
    out_refs, (done_ref, found_buf) = refs[SIDE + 2 : 2 * SIDE + 2], refs[2 * SIDE + 2 :]
    span = own_ref.shape[1]
    width = own_ref.shape[2]
    entries = LEVELS * span
    count = FRAMES * LEVELS
    members = SIDE * SIDE
    rows = members * count
    me = lax.axis_index("batch")

    pick = (iota((rows, members), 0) // count == iota((rows, members), 1)).astype(jnp.bfloat16)
    row = iota((rows, LEVELS), 0)
    lane = iota((rows, LEVELS), 1)
    block = jnp.zeros((rows, LEVELS), jnp.float32)
    inner = jnp.zeros((rows, LEVELS), jnp.float32)
    for f in range(FRAMES):
        ids = jnp.concatenate([ref[:, f, :] for ref in ids_refs], axis=0)
        mine = (lane == row % LEVELS) & ((row // LEVELS) % FRAMES == f)
        high = (ids // span).astype(jnp.float32).astype(jnp.bfloat16)
        low = (ids % span).astype(jnp.float32).astype(jnp.bfloat16)
        block = jnp.where(mine, dot_nn(pick, high), block)
        inner = jnp.where(mine, dot_nn(pick, low), inner)
    block = jnp.sum(block, axis=1, keepdims=True).astype(jnp.int32)
    inner = jnp.sum(inner, axis=1, keepdims=True).astype(jnp.int32)
    level = iota((rows, 1), 0) % LEVELS
    place = inner + level * span
    at_own = jnp.where(block == me, place, -1)
    at_other = jnp.where(block == (me ^ 1), place, -1)
    entry = iota((rows, entries), 1)
    hot_own = jnp.where(entry == at_own, 1.0, 0.0).astype(jnp.bfloat16)
    hot_other = jnp.where(entry == at_other, 1.0, 0.0).astype(jnp.bfloat16)
    found = dot_nn(hot_own, own_ref[...].reshape(entries, width))
    found = found + dot_nn(hot_other, other_ref[...].reshape(entries, width))
    found_buf[...] = found.astype(jnp.bfloat16).reshape(found_buf.shape)
    for s in range(SIDE):
        out_refs[s][...] = found_buf[s * SIDE : (s + 1) * SIDE]
    done_ref[...] = jnp.zeros_like(done_ref)


def collect_kernel(own_ref, *refs):
    arrived, out_refs = refs[: SIDE - 1], refs[SIDE - 1 :]
    for s in range(SIDE):
        value = own_ref[s]
        for ref in arrived:
            value = value + ref[s]
        out_refs[s][...] = value


def fetch_kernel(w_hbm, order_ref, out_ref, sem):
    copy = pltpu.make_async_copy(w_hbm, out_ref, sem)
    copy.start()
    copy.wait()


def middle_kernel(
    shares_ref, residual_ref, gain_ref, w_hbm, order_ref, stream_ref, sent_ref,
    w_ref, rows_buf, sent_buf, sem
):
    get_weight = pltpu.make_async_copy(w_hbm, w_ref, sem)
    get_weight.start()
    dialogues = residual_ref.shape[0]
    for d in range(dialogues):
        rows_buf[FRAMES * d : FRAMES * (d + 1), :] = residual_ref[d].astype(jnp.float32)
    hidden = rows_buf[...]
    share = shares_ref[0].astype(jnp.float32)
    for t in range(1, shares_ref.shape[0]):
        share = share + shares_ref[t].astype(jnp.float32)
    hidden = hidden + share
    rows_buf[...] = hidden
    squares = jnp.sum(hidden * hidden, axis=-1, keepdims=True)
    scaled = (hidden * gain_ref[...]).astype(jnp.bfloat16)
    width = w_ref.shape[1]
    sent_buf[:, width:] = jnp.broadcast_to(squares, (hidden.shape[0], EXTRA))
    for d in range(dialogues):
        stream_ref[d] = rows_buf[FRAMES * d : FRAMES * (d + 1), :].astype(jnp.bfloat16)
    get_weight.wait()
    sent_buf[:, :width] = dot_nn(scaled, w_ref[...])
    for d in range(dialogues):
        sent_ref[d] = sent_buf[FRAMES * d : FRAMES * (d + 1), :]


def depth_kernel(
    terms_ref, *refs
):
    table_refs = refs[:SIDE]
    gain_ref, qkv_ref, o_hbm, out_ref, o_ref, sem = refs[SIDE:]
    get_weight = pltpu.make_async_copy(o_hbm, o_ref, sem)
    get_weight.start()
    count, width = table_refs[0].shape
    terms = terms_ref[0]
    for t in range(1, terms_ref.shape[0]):
        terms = terms + terms_ref[t]
    inverse = lax.rsqrt(terms[:, width : width + 1] / D + 1e-05)
    proj = terms[:, :width] * inverse
    values = table_refs[0][...].astype(jnp.float32)
    for ref in table_refs[1:]:
        values = values + ref[...].astype(jnp.float32)
    frame = iota((count, width), 0) // LEVELS
    depth_input = values + jnp.where(frame == 0, proj[0:1], proj[1:2])
    mean = jnp.sum(depth_input * depth_input, axis=-1, keepdims=True) / width
    normed = (depth_input * lax.rsqrt(mean + 1e-05) * gain_ref[...]).astype(jnp.bfloat16)
    heads_width = DHEADS * DHD
    query = dot_nn(normed, qkv_ref[:, :heads_width]).astype(jnp.bfloat16).astype(jnp.float32)
    key = dot_nn(normed, qkv_ref[:, heads_width : 2 * heads_width]).astype(jnp.bfloat16)
    value = dot_nn(normed, qkv_ref[:, 2 * heads_width :]).astype(jnp.bfloat16)
    head_of = iota((count, heads_width), 1) // DHD
    spread = jnp.concatenate(
        [jnp.where(head_of == h, query, 0.0) for h in range(DHEADS)], axis=0
    ).astype(jnp.bfloat16)
    scores = dot_nt(spread, key) * (1.0 / math.sqrt(DHD))
    row = iota(scores.shape, 0) % count
    col = iota(scores.shape, 1)
    seen = (row // LEVELS == col // LEVELS) & (col <= row)
    exps = jnp.where(seen, jnp.exp(scores), 0.0)
    probs = (exps / jnp.sum(exps, axis=-1, keepdims=True)).astype(jnp.bfloat16)
    spread_out = dot_nn(probs, value)
    mixed = spread_out[:count]
    for h in range(1, DHEADS):
        mixed = jnp.where(head_of == h, spread_out[h * count : (h + 1) * count], mixed)
    get_weight.wait()
    out_ref[...] = (depth_input + dot_nn(mixed.astype(jnp.bfloat16), o_ref[...])).astype(
        jnp.bfloat16
    )


VMEM = pl.BlockSpec(memory_space=pltpu.VMEM)
SMEM = pl.BlockSpec(memory_space=pltpu.SMEM)
ANY = pl.BlockSpec(memory_space=pl.ANY)


def hbm(*arrays):
    return tuple(pltpu.with_memory_space_constraint(a, pltpu.HBM) for a in arrays)


def call(kernel, name, outs, ins, out_specs, scratch, limit, flops, moved):
    return pl.pallas_call(
        kernel,
        name=name,
        out_shape=outs,
        in_specs=ins,
        out_specs=out_specs,
        scratch_shapes=scratch,
        compiler_params=pltpu.CompilerParams(vmem_limit_bytes=limit * MIB),
        cost_estimate=pl.CostEstimate(flops=flops, bytes_accessed=moved, transcendentals=0),
    )


def flipped(size, step, s):
    span = SIDE * step
    return [(b, b // span * span + (b % span // step ^ s) * step + b % step) for b in range(size)]


def sorted_steps(arrays):
    return [arrays[STEPS.index(s)] for s in range(1, SIDE)]


def per_device(
    residual,
    new_queries,
    new_keys,
    new_values,
    cache_keys,
    cache_values,
    lengths,
    out_weight,
    temporal_gain,
    in_weight,
    tokens,
    level_tables,
    depth_gain,
    depth_qkv,
    depth_out,
):
    shape = jax.ShapeDtypeStruct
    bf16, f32 = jnp.bfloat16, jnp.float32
    held, _, features = residual.shape
    tensor_size = lax.axis_size("tensor")
    batch_size = lax.axis_size("batch")
    rows = held * FRAMES
    width = in_weight.shape[1]
    members = batch_size // CORES
    count = FRAMES * LEVELS

    other_tables = lax.ppermute(level_tables, "batch", flipped(batch_size, 1, 1))
    order = call(
        warm_kernel, "warm", pltpu.VMEM((8, 128), f32), [], VMEM, [], LIMIT, WARM_FLOPS, 1
    )()
    near = [lax.ppermute(tokens, "batch", flipped(batch_size, CORES, s)) for s in STEPS]
    head_terms, own_tables = call(
        attend_kernel,
        "attend",
        (
            pltpu.HBM((tensor_size, rows, features), bf16),
            pltpu.VMEM(level_tables.shape, bf16),
        ),
        [ANY] + [VMEM] * 4 + [ANY, VMEM, ANY, VMEM],
        (ANY, VMEM),
        [
            pltpu.SMEM((held,), jnp.int32),
            pltpu.VMEM(cache_values.shape, bf16),
            pltpu.VMEM((3, rows, new_queries.shape[2]), f32),
            pltpu.VMEM((tensor_size, rows, features), bf16),
            pltpu.SemaphoreType.DMA((3 + tensor_size,)),
        ],
        LIMIT,
        10**8,
        4 * 2**20,
    )(
        *hbm(lengths),
        new_queries,
        new_keys,
        new_values,
        cache_keys,
        *hbm(cache_values),
        out_weight,
        *hbm(level_tables),
        order,
    )
    column = call(
        gather_kernel,
        "gather",
        pltpu.VMEM((SIDE, FRAMES, LEVELS), jnp.int32),
        [VMEM] * (SIDE + 1),
        VMEM,
        [],
        LIMIT,
        10**6,
        1,
    )(tokens, *sorted_steps(near), own_tables)
    ids = [lax.ppermute(column, "batch", flipped(batch_size, CORES * SIDE, s)) for s in STEPS]

    shares = lax.all_to_all(head_terms, "tensor", 0, 0, tiled=True)

    *partial_rows, looked = call(
        lookup_kernel,
        "lookup",
        (
            *[pltpu.VMEM((SIDE, count, width), bf16)] * SIDE,
            pltpu.VMEM((8, 128), f32),
        ),
        [VMEM] * (SIDE + 2),
        (VMEM,) * (SIDE + 1),
        [
            pltpu.VMEM((members, count, width), bf16),
        ],
        LIMIT,
        10**11,
        1,
    )(column, *sorted_steps(ids), own_tables, other_tables)
    across = [
        lax.ppermute(partial_rows[s], "batch", flipped(batch_size, CORES * SIDE, s))
        for s in STEPS
    ]
    own_rows, *side_rows = call(
        collect_kernel,
        "collect",
        [pltpu.VMEM((count, width), bf16)] * SIDE,
        [VMEM] * SIDE,
        [VMEM] * SIDE,
        [],
        LIMIT,
        10**6,
        1,
    )(partial_rows[0], *across)
    along = [
        lax.ppermute(side_rows[s - 1], "batch", flipped(batch_size, CORES, s)) for s in STEPS
    ]

    temporal_out, sent = call(
        middle_kernel,
        "middle",
        (pltpu.HBM(residual.shape, bf16), pltpu.HBM((held, FRAMES, width + EXTRA), f32)),
        [VMEM] * 3 + [ANY, VMEM],
        (VMEM, VMEM),
        [
            pltpu.VMEM(in_weight.shape, bf16),
            pltpu.VMEM((rows, features), f32),
            pltpu.VMEM((rows, width + EXTRA), f32),
            pltpu.SemaphoreType.DMA,
        ],
        LIMIT,
        10**9,
        1,
    )(shares, residual, temporal_gain.astype(f32).reshape(1, features), *hbm(in_weight), looked)
    terms = lax.all_to_all(sent, "tensor", 0, 0, tiled=True)

    qkv_near = call(
        fetch_kernel,
        "fetch",
        pltpu.VMEM(depth_qkv.shape, bf16),
        [ANY, VMEM],
        VMEM,
        [pltpu.SemaphoreType.DMA],
        LIMIT,
        10**9,
        1,
    )(*hbm(depth_qkv), own_rows)
    states = call(
        depth_kernel,
        "depth",
        pltpu.HBM((count, width), bf16),
        [VMEM] * (SIDE + 3) + [ANY],
        VMEM,
        [pltpu.VMEM(depth_out.shape, bf16), pltpu.SemaphoreType.DMA],
        LIMIT,
        10**9,
        1,
    )(terms, own_rows, *along, depth_gain.astype(f32).reshape(1, width), qkv_near, *hbm(depth_out))
    return (temporal_out, states.reshape(1, FRAMES, LEVELS, width))


def solution(mesh):
    placed = (
        P("batch", None, "tensor"),
        P("batch", None, "tensor"),
        P("batch", None, "tensor"),
        P("batch", None, "tensor"),
        P("batch", None, "tensor"),
        P("batch", None, "tensor"),
        P("batch"),
        P("tensor", None),
        P("tensor"),
        P("tensor", None),
        P(("batch", "tensor"), None, None),
        P(None, "batch", None),
        P(),
        P(),
        P(),
    )
    return jax.shard_map(
        per_device,
        mesh=mesh,
        in_specs=placed,
        out_specs=(P("batch", None, "tensor"), P(("batch", "tensor"), None, None, None)),
        check_vma=False,
    )
```

```python
import functools
import math

import jax
import jax.numpy as jnp
from jax import lax
from jax.experimental import pallas as pl
from jax.experimental.pallas import tpu as pltpu
from jax.sharding import PartitionSpec as P

D = 4096
HD = 128
DD = 1024
DHD = 64
DHEADS = 8
LEVELS = 8
FRAMES = 2
CORES = 2
SIDE = 4
STEPS = (2, 1, 3)
LATE = 256
EXTRA = 128
MIB = 2**20
LIMIT = 16
WARM_FLOPS = 10**10
NT = (((1,), (1,)), ((), ()))


def dot_nt(a, b):
    return lax.dot_general(a, b, NT, preferred_element_type=jnp.float32)


def dot_nn(a, b):
    return jnp.dot(a, b, preferred_element_type=jnp.float32)


def iota(shape, axis):
    return lax.broadcasted_iota(jnp.int32, shape, axis)


def warm_kernel(*refs):
    refs[-1][...] = jnp.zeros_like(refs[-1])


def attend_kernel(
    lengths_hbm, q_ref, nk_ref, nv_ref, k_ref, v_hbm, w_ref, own_hbm, order_ref, out_hbm, own_ref,
    lengths_buf, v_buf, small, sent_buf, sems
):
    get_lengths = pltpu.make_async_copy(lengths_hbm, lengths_buf, sems.at[0])
    dialogues = q_ref.shape[0]
    half = dialogues // 2
    get_values = [
        pltpu.make_async_copy(
            v_hbm.at[pl.ds(i * half, half)], v_buf.at[pl.ds(i * half, half)], sems.at[1 + i]
        )
        for i in range(2)
    ]
    get_own = pltpu.make_async_copy(own_hbm, own_ref, sems.at[3])
    get_lengths.start()
    get_values[0].start()
    get_values[1].start()
    width = q_ref.shape[2]
    rows = dialogues * FRAMES
    heads = width // HD
    stacked = heads * rows
    slots = k_ref.shape[1]
    for i, ref in enumerate((q_ref, nk_ref, nv_ref)):
        for d in range(dialogues):
            small[i, FRAMES * d : FRAMES * (d + 1), :] = ref[d].astype(jnp.float32)
    query = small[0]
    fresh_key = small[1].astype(jnp.bfloat16)
    fresh_value = small[2].astype(jnp.bfloat16)
    head_of = iota((rows, width), 1) // HD
    spread = jnp.concatenate(
        [jnp.where(head_of == h, query, 0.0) for h in range(heads)], axis=0
    ).astype(jnp.bfloat16)
    scale = 1.0 / math.sqrt(HD)

    slot = iota((stacked, slots), 1)
    dialogue = (iota((stacked, slots), 0) % rows) // FRAMES
    of_dialogue = [dialogue == d for d in range(dialogues)]
    scores = jnp.zeros((stacked, slots), jnp.float32)
    for d in range(dialogues):
        scores = jnp.where(of_dialogue[d], dot_nt(spread, k_ref[d]), scores)
    row_n = iota((stacked, rows), 0) % rows
    col_n = iota((stacked, rows), 1)
    seen = (row_n // FRAMES == col_n // FRAMES) & (col_n <= row_n)
    fresh = jnp.where(seen, dot_nt(spread, fresh_key) * scale, -jnp.inf)
    get_lengths.wait()
    live = jnp.zeros((stacked, slots), jnp.int32)
    for d in range(dialogues):
        live = jnp.where(of_dialogue[d], lengths_buf[d], live)
    scores = jnp.where(slot < live, scores * scale, -jnp.inf)
    largest = jnp.maximum(
        jnp.max(scores, axis=-1, keepdims=True), jnp.max(fresh, axis=-1, keepdims=True)
    )
    exp_cache = jnp.exp(scores - largest)
    exp_fresh = jnp.exp(fresh - largest)
    total = jnp.sum(exp_cache, axis=-1, keepdims=True) + jnp.sum(
        exp_fresh, axis=-1, keepdims=True
    )
    mixed = dot_nn(exp_fresh.astype(jnp.bfloat16), fresh_value)
    for d in range(dialogues):
        if d % half == 0:
            get_values[d // half].wait()
        own = jnp.where(of_dialogue[d], exp_cache, 0.0).astype(jnp.bfloat16)
        mixed = mixed + dot_nn(own, v_buf[d])
    get_own.start()
    mixed = mixed / total
    attended = mixed[:rows]
    for h in range(1, heads):
        attended = jnp.where(head_of == h, mixed[h * rows : (h + 1) * rows], attended)
    attended = attended.astype(jnp.bfloat16)
    peers, _, features = sent_buf.shape
    sends = []
    for t in range(peers):
        sent_buf[t] = dot_nn(attended, w_ref[:, t * features : (t + 1) * features]).astype(
            jnp.bfloat16
        )
        sends.append(pltpu.make_async_copy(sent_buf.at[t], out_hbm.at[t], sems.at[4 + t]))
        sends[t].start()
    get_own.wait()
    for send in sends:
        send.wait()


def gather_kernel(*refs):
    out_ref = refs[-1]
    for i in range(SIDE):
        out_ref[i] = refs[i][0]


def lookup_kernel(*refs):
    ids_refs, (own_ref, other_ref) = refs[:SIDE], refs[SIDE : SIDE + 2]
    out_refs, found_buf = refs[SIDE + 2 : 2 * SIDE + 2], refs[-1]
    span = own_ref.shape[1]
    width = own_ref.shape[2]
    entries = LEVELS * span
    count = FRAMES * LEVELS
    members = SIDE * SIDE
    rows = members * count
    me = lax.axis_index("batch")

    pick = (iota((rows, members), 0) // count == iota((rows, members), 1)).astype(jnp.bfloat16)
    row = iota((rows, LEVELS), 0)
    lane = iota((rows, LEVELS), 1)
    block = jnp.zeros((rows, LEVELS), jnp.float32)
    inner = jnp.zeros((rows, LEVELS), jnp.float32)
    for f in range(FRAMES):
        ids = jnp.concatenate([ref[:, f, :] for ref in ids_refs], axis=0)
        mine = (lane == row % LEVELS) & ((row // LEVELS) % FRAMES == f)
        high = (ids // span).astype(jnp.float32).astype(jnp.bfloat16)
        low = (ids % span).astype(jnp.float32).astype(jnp.bfloat16)
        block = jnp.where(mine, dot_nn(pick, high), block)
        inner = jnp.where(mine, dot_nn(pick, low), inner)
    block = jnp.sum(block, axis=1, keepdims=True).astype(jnp.int32)
    inner = jnp.sum(inner, axis=1, keepdims=True).astype(jnp.int32)
    level = iota((rows, 1), 0) % LEVELS
    place = inner + level * span
    at_own = jnp.where(block == me, place, -1)
    at_other = jnp.where(block == (me ^ 1), place, -1)
    entry = iota((rows, entries), 1)
    hot_own = jnp.where(entry == at_own, 1.0, 0.0).astype(jnp.bfloat16)
    hot_other = jnp.where(entry == at_other, 1.0, 0.0).astype(jnp.bfloat16)
    found = dot_nn(hot_own, own_ref[...].reshape(entries, width))
    found = found + dot_nn(hot_other, other_ref[...].reshape(entries, width))
    found_buf[...] = found.astype(jnp.bfloat16).reshape(found_buf.shape)
    for s in range(SIDE):
        out_refs[s][...] = found_buf[s * SIDE : (s + 1) * SIDE]


def collect_kernel(own_ref, *refs):
    arrived, out_refs = refs[: SIDE - 1], refs[SIDE - 1 :]
    for s in range(SIDE):
        value = own_ref[s]
        for ref in arrived:
            value = value + ref[s]
        out_refs[s][...] = value


def fetch_kernel(qkv_hbm, o_hbm, order_ref, out_ref, sems):
    near = qkv_hbm.shape[1] - LATE
    copies = [
        pltpu.make_async_copy(qkv_hbm.at[:, pl.ds(0, near)], out_ref.at[:, pl.ds(0, near)], sems.at[0])
    ]
    for j in range(o_hbm.shape[1] // LATE):
        part = pl.ds(j * LATE, LATE)
        copies.append(
            pltpu.make_async_copy(
                o_hbm.at[pl.ds(0, LATE), part], out_ref.at[part, pl.ds(near, LATE)], sems.at[1 + j]
            )
        )
    for copy in copies:
        copy.start()
    for copy in copies:
        copy.wait()


def middle_kernel(
    shares_ref, residual_ref, gain_ref, w_ref, order_ref, stream_ref, sent_ref, rows_buf, sent_buf
):
    dialogues = residual_ref.shape[0]
    for d in range(dialogues):
        rows_buf[FRAMES * d : FRAMES * (d + 1), :] = residual_ref[d].astype(jnp.float32)
    hidden = rows_buf[...]
    share = shares_ref[0].astype(jnp.float32)
    for t in range(1, shares_ref.shape[0]):
        share = share + shares_ref[t].astype(jnp.float32)
    hidden = hidden + share
    rows_buf[...] = hidden
    squares = jnp.sum(hidden * hidden, axis=-1, keepdims=True)
    scaled = (hidden * gain_ref[...]).astype(jnp.bfloat16)
    width = w_ref.shape[1]
    sent_buf[:, width:] = jnp.broadcast_to(squares, (hidden.shape[0], EXTRA))
    for d in range(dialogues):
        stream_ref[d] = rows_buf[FRAMES * d : FRAMES * (d + 1), :].astype(jnp.bfloat16)
    sent_buf[:, :width] = dot_nn(scaled, w_ref[...])
    for d in range(dialogues):
        sent_ref[d] = sent_buf[FRAMES * d : FRAMES * (d + 1), :]


def depth_kernel(
    terms_ref, *refs
):
    table_refs = refs[:SIDE]
    gain_ref, near_ref, qkv_hbm, o_hbm, out_ref, v_buf, o_buf, sems = refs[SIDE:]
    heads_width = DHEADS * DHD
    near = 3 * heads_width - LATE
    get_v = pltpu.make_async_copy(qkv_hbm.at[:, pl.ds(near, LATE)], v_buf, sems.at[0])
    get_o = pltpu.make_async_copy(
        o_hbm.at[pl.ds(heads_width - LATE, LATE)], o_buf, sems.at[1]
    )
    get_v.start()
    get_o.start()
    count, width = table_refs[0].shape
    terms = terms_ref[0]
    for t in range(1, terms_ref.shape[0]):
        terms = terms + terms_ref[t]
    inverse = lax.rsqrt(terms[:, width : width + 1] / D + 1e-05)
    proj = terms[:, :width] * inverse
    values = table_refs[0][...].astype(jnp.float32)
    for ref in table_refs[1:]:
        values = values + ref[...].astype(jnp.float32)
    frame = iota((count, width), 0) // LEVELS
    depth_input = values + jnp.where(frame == 0, proj[0:1], proj[1:2])
    mean = jnp.sum(depth_input * depth_input, axis=-1, keepdims=True) / width
    normed = (depth_input * lax.rsqrt(mean + 1e-05) * gain_ref[...]).astype(jnp.bfloat16)
    query = dot_nn(normed, near_ref[:, :heads_width]).astype(jnp.bfloat16).astype(jnp.float32)
    key = dot_nn(normed, near_ref[:, heads_width : 2 * heads_width]).astype(jnp.bfloat16)
    value = dot_nn(normed, near_ref[:, 2 * heads_width : near]).astype(jnp.bfloat16)
    head_of = iota((count, heads_width), 1) // DHD
    spread = jnp.concatenate(
        [jnp.where(head_of == h, query, 0.0) for h in range(DHEADS)], axis=0
    ).astype(jnp.bfloat16)
    scores = dot_nt(spread, key) * (1.0 / math.sqrt(DHD))
    row = iota(scores.shape, 0) % count
    col = iota(scores.shape, 1)
    seen = (row // LEVELS == col // LEVELS) & (col <= row)
    exps = jnp.where(seen, jnp.exp(scores), 0.0)
    probs = (exps / jnp.sum(exps, axis=-1, keepdims=True)).astype(jnp.bfloat16)
    get_v.wait()
    late_value = dot_nn(normed, v_buf[...]).astype(jnp.bfloat16)
    spread_out = dot_nn(probs, jnp.concatenate([value, late_value], axis=1))
    mixed = spread_out[:count]
    for h in range(1, DHEADS):
        mixed = jnp.where(head_of == h, spread_out[h * count : (h + 1) * count], mixed)
    mixed = mixed.astype(jnp.bfloat16)
    early = jnp.concatenate(
        [
            dot_nn(mixed[:, :LATE], near_ref[j * LATE : (j + 1) * LATE, near:])
            for j in range(width // LATE)
        ],
        axis=1,
    )
    get_o.wait()
    late = dot_nn(mixed[:, LATE:], o_buf[...])
    out_ref[...] = (depth_input + early + late).astype(jnp.bfloat16)


VMEM = pl.BlockSpec(memory_space=pltpu.VMEM)
SMEM = pl.BlockSpec(memory_space=pltpu.SMEM)
ANY = pl.BlockSpec(memory_space=pl.ANY)


def hbm(*arrays):
    return tuple(pltpu.with_memory_space_constraint(a, pltpu.HBM) for a in arrays)


def call(kernel, name, outs, ins, out_specs, scratch, limit, flops, moved):
    return pl.pallas_call(
        kernel,
        name=name,
        out_shape=outs,
        in_specs=ins,
        out_specs=out_specs,
        scratch_shapes=scratch,
        compiler_params=pltpu.CompilerParams(vmem_limit_bytes=limit * MIB),
        cost_estimate=pl.CostEstimate(flops=flops, bytes_accessed=moved, transcendentals=0),
    )


def flipped(size, step, s):
    span = SIDE * step
    return [(b, b // span * span + (b % span // step ^ s) * step + b % step) for b in range(size)]


def sorted_steps(arrays):
    return [arrays[STEPS.index(s)] for s in range(1, SIDE)]


def per_device(
    residual,
    new_queries,
    new_keys,
    new_values,
    cache_keys,
    cache_values,
    lengths,
    out_weight,
    temporal_gain,
    in_weight,
    tokens,
    level_tables,
    depth_gain,
    depth_qkv,
    depth_out,
):
    shape = jax.ShapeDtypeStruct
    bf16, f32 = jnp.bfloat16, jnp.float32
    held, _, features = residual.shape
    tensor_size = lax.axis_size("tensor")
    batch_size = lax.axis_size("batch")
    rows = held * FRAMES
    width = in_weight.shape[1]
    members = batch_size // CORES
    count = FRAMES * LEVELS

    order = call(
        warm_kernel, "warm", pltpu.VMEM((8, 128), f32), [], VMEM, [], LIMIT, WARM_FLOPS, 1
    )()
    other_tables = lax.ppermute(level_tables, "batch", flipped(batch_size, 1, 1))
    near = [lax.ppermute(tokens, "batch", flipped(batch_size, CORES, s)) for s in STEPS]
    head_terms, own_tables = call(
        attend_kernel,
        "attend",
        (
            pltpu.HBM((tensor_size, rows, features), bf16),
            pltpu.VMEM(level_tables.shape, bf16),
        ),
        [ANY] + [VMEM] * 4 + [ANY, VMEM, ANY, VMEM],
        (ANY, VMEM),
        [
            pltpu.SMEM((held,), jnp.int32),
            pltpu.VMEM(cache_values.shape, bf16),
            pltpu.VMEM((3, rows, new_queries.shape[2]), f32),
            pltpu.VMEM((tensor_size, rows, features), bf16),
            pltpu.SemaphoreType.DMA((4 + tensor_size,)),
        ],
        LIMIT,
        10**8,
        4 * 2**20,
    )(
        *hbm(lengths),
        new_queries,
        new_keys,
        new_values,
        cache_keys,
        *hbm(cache_values),
        out_weight,
        *hbm(level_tables),
        order,
    )
    column = call(
        gather_kernel,
        "gather",
        pltpu.VMEM((SIDE, FRAMES, LEVELS), jnp.int32),
        [VMEM] * (SIDE + 1),
        VMEM,
        [],
        LIMIT,
        10**6,
        1,
    )(tokens, *sorted_steps(near), own_tables)
    ids = [lax.ppermute(column, "batch", flipped(batch_size, CORES * SIDE, s)) for s in STEPS]

    shares = lax.all_to_all(head_terms, "tensor", 0, 0, tiled=True)

    partial_rows = call(
        lookup_kernel,
        "lookup",
        [pltpu.VMEM((SIDE, count, width), bf16)] * SIDE,
        [VMEM] * (SIDE + 2),
        [VMEM] * SIDE,
        [
            pltpu.VMEM((members, count, width), bf16),
        ],
        LIMIT,
        10**11,
        1,
    )(column, *sorted_steps(ids), own_tables, other_tables)
    looked = call(
        warm_kernel, "warm_in", pltpu.VMEM((8, 128), f32), [VMEM], VMEM, [], LIMIT, WARM_FLOPS, 1
    )(partial_rows[0])
    *partial_rows, looked = lax.optimization_barrier((*partial_rows, looked))
    across = [
        lax.ppermute(partial_rows[s], "batch", flipped(batch_size, CORES * SIDE, s))
        for s in STEPS
    ]
    own_rows, *side_rows = call(
        collect_kernel,
        "collect",
        [pltpu.VMEM((count, width), bf16)] * SIDE,
        [VMEM] * SIDE,
        [VMEM] * SIDE,
        [],
        LIMIT,
        10**6,
        1,
    )(partial_rows[0], *across)
    along = [
        lax.ppermute(side_rows[s - 1], "batch", flipped(batch_size, CORES, s)) for s in STEPS
    ]

    temporal_out, sent = call(
        middle_kernel,
        "middle",
        (pltpu.HBM(residual.shape, bf16), pltpu.HBM((held, FRAMES, width + EXTRA), f32)),
        [VMEM] * 5,
        (VMEM, VMEM),
        [
            pltpu.VMEM((rows, features), f32),
            pltpu.VMEM((rows, width + EXTRA), f32),
        ],
        LIMIT,
        10**9,
        1,
    )(shares, residual, temporal_gain.astype(f32).reshape(1, features), in_weight, looked)
    terms = lax.all_to_all(sent, "tensor", 0, 0, tiled=True)

    near_weights = call(
        fetch_kernel,
        "fetch",
        pltpu.VMEM(depth_qkv.shape, bf16),
        [ANY, ANY, VMEM],
        VMEM,
        [pltpu.SemaphoreType.DMA((1 + width // LATE,))],
        LIMIT,
        10**9,
        1,
    )(*hbm(depth_qkv, depth_out), own_rows)
    states = call(
        depth_kernel,
        "depth",
        pltpu.HBM((count, width), bf16),
        [VMEM] * (SIDE + 3) + [ANY, ANY],
        VMEM,
        [
            pltpu.VMEM((width, LATE), bf16),
            pltpu.VMEM((LATE, width), bf16),
            pltpu.SemaphoreType.DMA((2,)),
        ],
        LIMIT,
        10**9,
        1,
    )(terms, own_rows, *along, depth_gain.astype(f32).reshape(1, width), near_weights, *hbm(depth_qkv, depth_out))
    return (temporal_out, states.reshape(1, FRAMES, LEVELS, width))


def solution(mesh):
    placed = (
        P("batch", None, "tensor"),
        P("batch", None, "tensor"),
        P("batch", None, "tensor"),
        P("batch", None, "tensor"),
        P("batch", None, "tensor"),
        P("batch", None, "tensor"),
        P("batch"),
        P("tensor", None),
        P("tensor"),
        P("tensor", None),
        P(("batch", "tensor"), None, None),
        P(None, "batch", None),
        P(),
        P(),
        P(),
    )
    return jax.shard_map(
        per_device,
        mesh=mesh,
        in_specs=placed,
        out_specs=(P("batch", None, "tensor"), P(("batch", "tensor"), None, None, None)),
        check_vma=False,
    )
```

```python
import functools
import math

import jax
import jax.numpy as jnp
from jax import lax
from jax.experimental import pallas as pl
from jax.experimental.pallas import tpu as pltpu
from jax.sharding import PartitionSpec as P

D = 4096
HD = 128
DD = 1024
DHD = 64
DHEADS = 8
LEVELS = 8
FRAMES = 2
CORES = 2
SIDE = 4
STEPS = (2, 1, 3)
LATE = 128
EXTRA = 128
MIB = 2**20
LIMIT = 16
WARM_FLOPS = 10**10
GATHER_FLOPS = 10**10
NT = (((1,), (1,)), ((), ()))


def dot_nt(a, b):
    return lax.dot_general(a, b, NT, preferred_element_type=jnp.float32)


def dot_nn(a, b):
    return jnp.dot(a, b, preferred_element_type=jnp.float32)


def iota(shape, axis):
    return lax.broadcasted_iota(jnp.int32, shape, axis)


def warm_kernel(*refs):
    refs[-1][...] = jnp.zeros_like(refs[-1])


def attend_kernel(
    lengths_hbm, q_ref, nk_ref, nv_ref, k_ref, v_ref, w_ref, order_ref, out_hbm, lengths_buf, small, sent_buf, sems
):
    get_lengths = pltpu.make_async_copy(lengths_hbm, lengths_buf, sems.at[0])
    dialogues = q_ref.shape[0]
    get_lengths.start()
    width = q_ref.shape[2]
    rows = dialogues * FRAMES
    heads = width // HD
    stacked = heads * rows
    slots = k_ref.shape[1]
    for i, ref in enumerate((q_ref, nk_ref, nv_ref)):
        for d in range(dialogues):
            small[i, FRAMES * d : FRAMES * (d + 1), :] = ref[d].astype(jnp.float32)
    query = small[0]
    fresh_key = small[1].astype(jnp.bfloat16)
    fresh_value = small[2].astype(jnp.bfloat16)
    head_of = iota((rows, width), 1) // HD
    spread = jnp.concatenate(
        [jnp.where(head_of == h, query, 0.0) for h in range(heads)], axis=0
    ).astype(jnp.bfloat16)
    scale = 1.0 / math.sqrt(HD)

    slot = iota((stacked, slots), 1)
    dialogue = (iota((stacked, slots), 0) % rows) // FRAMES
    of_dialogue = [dialogue == d for d in range(dialogues)]
    scores = jnp.zeros((stacked, slots), jnp.float32)
    for d in range(dialogues):
        scores = jnp.where(of_dialogue[d], dot_nt(spread, k_ref[d]), scores)
    row_n = iota((stacked, rows), 0) % rows
    col_n = iota((stacked, rows), 1)
    seen = (row_n // FRAMES == col_n // FRAMES) & (col_n <= row_n)
    fresh = jnp.where(seen, dot_nt(spread, fresh_key) * scale, -jnp.inf)
    get_lengths.wait()
    live = jnp.zeros((stacked, slots), jnp.int32)
    for d in range(dialogues):
        live = jnp.where(of_dialogue[d], lengths_buf[d], live)
    scores = jnp.where(slot < live, scores * scale, -jnp.inf)
    largest = jnp.maximum(
        jnp.max(scores, axis=-1, keepdims=True), jnp.max(fresh, axis=-1, keepdims=True)
    )
    exp_cache = jnp.exp(scores - largest)
    exp_fresh = jnp.exp(fresh - largest)
    total = jnp.sum(exp_cache, axis=-1, keepdims=True) + jnp.sum(
        exp_fresh, axis=-1, keepdims=True
    )
    mixed = dot_nn(exp_fresh.astype(jnp.bfloat16), fresh_value)
    for d in range(dialogues):
        own = jnp.where(of_dialogue[d], exp_cache, 0.0).astype(jnp.bfloat16)
        mixed = mixed + dot_nn(own, v_ref[d])
    mixed = mixed / total
    attended = mixed[:rows]
    for h in range(1, heads):
        attended = jnp.where(head_of == h, mixed[h * rows : (h + 1) * rows], attended)
    attended = attended.astype(jnp.bfloat16)
    peers, _, features = sent_buf.shape
    sends = []
    for t in range(peers):
        sent_buf[t] = dot_nn(attended, w_ref[:, t * features : (t + 1) * features]).astype(
            jnp.bfloat16
        )
        sends.append(pltpu.make_async_copy(sent_buf.at[t], out_hbm.at[peers - 1 - t], sems.at[3 + t]))
        sends[t].start()
    for send in sends:
        send.wait()


def gather_kernel(*refs):
    out_ref = refs[-1]
    for i in range(SIDE):
        out_ref[i] = refs[i][0]


def lookup_kernel(*refs):
    ids_refs, (own_ref, other_ref) = refs[:SIDE], refs[SIDE : SIDE + 2]
    out_refs, found_buf = refs[SIDE + 2 : 2 * SIDE + 2], refs[-1]
    span = own_ref.shape[1]
    width = own_ref.shape[2]
    entries = LEVELS * span
    count = FRAMES * LEVELS
    members = SIDE * SIDE
    rows = members * count
    me = lax.axis_index("batch")

    pick = (iota((rows, members), 0) // count == iota((rows, members), 1)).astype(jnp.bfloat16)
    row = iota((rows, LEVELS), 0)
    lane = iota((rows, LEVELS), 1)
    block = jnp.zeros((rows, LEVELS), jnp.float32)
    inner = jnp.zeros((rows, LEVELS), jnp.float32)
    for f in range(FRAMES):
        ids = jnp.concatenate([ref[:, f, :] for ref in ids_refs], axis=0)
        mine = (lane == row % LEVELS) & ((row // LEVELS) % FRAMES == f)
        high = (ids // span).astype(jnp.float32).astype(jnp.bfloat16)
        low = (ids % span).astype(jnp.float32).astype(jnp.bfloat16)
        block = jnp.where(mine, dot_nn(pick, high), block)
        inner = jnp.where(mine, dot_nn(pick, low), inner)
    block = jnp.sum(block, axis=1, keepdims=True).astype(jnp.int32)
    inner = jnp.sum(inner, axis=1, keepdims=True).astype(jnp.int32)
    level = iota((rows, 1), 0) % LEVELS
    place = inner + level * span
    at_own = jnp.where(block == me, place, -1)
    at_other = jnp.where(block == (me ^ 1), place, -1)
    entry = iota((rows, entries), 1)
    hot_own = jnp.where(entry == at_own, 1.0, 0.0).astype(jnp.bfloat16)
    hot_other = jnp.where(entry == at_other, 1.0, 0.0).astype(jnp.bfloat16)
    found = dot_nn(hot_own, own_ref[...].reshape(entries, width))
    found = found + dot_nn(hot_other, other_ref[...].reshape(entries, width))
    found_buf[...] = found.astype(jnp.bfloat16).reshape(found_buf.shape)
    for s in range(SIDE):
        out_refs[s][...] = found_buf[s * SIDE : (s + 1) * SIDE]


def collect_kernel(own_ref, *refs):
    arrived, out_refs = refs[: SIDE - 1], refs[SIDE - 1 :]
    for s in range(SIDE):
        value = own_ref[s]
        for ref in arrived:
            value = value + ref[s]
        out_refs[s][...] = value


def fetch_kernel(qkv_hbm, o_hbm, order_ref, out_ref, sems):
    near = qkv_hbm.shape[1] - LATE
    copies = [
        pltpu.make_async_copy(qkv_hbm.at[:, pl.ds(0, near)], out_ref.at[:, pl.ds(0, near)], sems.at[0])
    ]
    for j in range(o_hbm.shape[1] // LATE):
        part = pl.ds(j * LATE, LATE)
        copies.append(
            pltpu.make_async_copy(
                o_hbm.at[pl.ds(0, LATE), part], out_ref.at[part, pl.ds(near, LATE)], sems.at[1 + j]
            )
        )
    for copy in copies:
        copy.start()
    for copy in copies:
        copy.wait()


def middle_kernel(
    shares_ref, residual_ref, gain_ref, w_ref, order_ref, stream_ref, sent_ref, rows_buf, sent_buf
):
    dialogues = residual_ref.shape[0]
    for d in range(dialogues):
        rows_buf[FRAMES * d : FRAMES * (d + 1), :] = residual_ref[d].astype(jnp.float32)
    hidden = rows_buf[...]
    share = shares_ref[0].astype(jnp.float32)
    for t in range(1, shares_ref.shape[0]):
        share = share + shares_ref[t].astype(jnp.float32)
    hidden = hidden + share
    rows_buf[...] = hidden
    squares = jnp.sum(hidden * hidden, axis=-1, keepdims=True)
    scaled = (hidden * gain_ref[...]).astype(jnp.bfloat16)
    width = w_ref.shape[1]
    sent_buf[:, width:] = jnp.broadcast_to(squares, (hidden.shape[0], EXTRA))
    for d in range(dialogues):
        stream_ref[d] = rows_buf[FRAMES * d : FRAMES * (d + 1), :].astype(jnp.bfloat16)
    sent_buf[:, :width] = dot_nn(scaled, w_ref[...])
    for d in range(dialogues):
        sent_ref[dialogues - 1 - d] = sent_buf[FRAMES * d : FRAMES * (d + 1), :]


def depth_kernel(
    terms_ref, *refs
):
    table_refs = refs[:SIDE]
    gain_ref, near_ref, qkv_hbm, o_hbm, out_ref, v_buf, o_buf, sems = refs[SIDE:]
    heads_width = DHEADS * DHD
    near = 3 * heads_width - LATE
    get_v = pltpu.make_async_copy(qkv_hbm.at[:, pl.ds(near, LATE)], v_buf, sems.at[0])
    get_o = pltpu.make_async_copy(
        o_hbm.at[pl.ds(LATE, heads_width - LATE)], o_buf, sems.at[1]
    )
    get_v.start()
    get_o.start()
    count, width = table_refs[0].shape
    terms = terms_ref[0]
    for t in range(1, terms_ref.shape[0]):
        terms = terms + terms_ref[t]
    inverse = lax.rsqrt(terms[:, width : width + 1] / D + 1e-05)
    proj = terms[:, :width] * inverse
    values = table_refs[0][...].astype(jnp.float32)
    for ref in table_refs[1:]:
        values = values + ref[...].astype(jnp.float32)
    frame = iota((count, width), 0) // LEVELS
    depth_input = values + jnp.where(frame == 0, proj[0:1], proj[1:2])
    mean = jnp.sum(depth_input * depth_input, axis=-1, keepdims=True) / width
    normed = (depth_input * lax.rsqrt(mean + 1e-05) * gain_ref[...]).astype(jnp.bfloat16)
    query = dot_nn(normed, near_ref[:, :heads_width]).astype(jnp.bfloat16).astype(jnp.float32)
    key = dot_nn(normed, near_ref[:, heads_width : 2 * heads_width]).astype(jnp.bfloat16)
    value = dot_nn(normed, near_ref[:, 2 * heads_width : near]).astype(jnp.bfloat16)
    head_of = iota((count, heads_width), 1) // DHD
    spread = jnp.concatenate(
        [jnp.where(head_of == h, query, 0.0) for h in range(DHEADS)], axis=0
    ).astype(jnp.bfloat16)
    scores = dot_nt(spread, key) * (1.0 / math.sqrt(DHD))
    row = iota(scores.shape, 0) % count
    col = iota(scores.shape, 1)
    seen = (row // LEVELS == col // LEVELS) & (col <= row)
    exps = jnp.where(seen, jnp.exp(scores), 0.0)
    probs = (exps / jnp.sum(exps, axis=-1, keepdims=True)).astype(jnp.bfloat16)
    get_v.wait()
    late_value = dot_nn(normed, v_buf[...]).astype(jnp.bfloat16)
    spread_out = dot_nn(probs, jnp.concatenate([value, late_value], axis=1))
    mixed = spread_out[:count]
    for h in range(1, DHEADS):
        mixed = jnp.where(head_of == h, spread_out[h * count : (h + 1) * count], mixed)
    mixed = mixed.astype(jnp.bfloat16)
    early = jnp.concatenate(
        [
            dot_nn(mixed[:, :LATE], near_ref[j * LATE : (j + 1) * LATE, near:])
            for j in range(width // LATE)
        ],
        axis=1,
    )
    get_o.wait()
    late = dot_nn(mixed[:, LATE:], o_buf[...])
    out_ref[...] = (depth_input + early + late).astype(jnp.bfloat16)


VMEM = pl.BlockSpec(memory_space=pltpu.VMEM)
SMEM = pl.BlockSpec(memory_space=pltpu.SMEM)
ANY = pl.BlockSpec(memory_space=pl.ANY)


def hbm(*arrays):
    return tuple(pltpu.with_memory_space_constraint(a, pltpu.HBM) for a in arrays)


def call(kernel, name, outs, ins, out_specs, scratch, limit, flops, moved):
    return pl.pallas_call(
        kernel,
        name=name,
        out_shape=outs,
        in_specs=ins,
        out_specs=out_specs,
        scratch_shapes=scratch,
        compiler_params=pltpu.CompilerParams(vmem_limit_bytes=limit * MIB),
        cost_estimate=pl.CostEstimate(flops=flops, bytes_accessed=moved, transcendentals=0),
    )


def flipped(size, step, s):
    span = SIDE * step
    return [(b, b // span * span + (b % span // step ^ s) * step + b % step) for b in range(size)]


def sorted_steps(arrays):
    return [arrays[STEPS.index(s)] for s in range(1, SIDE)]


def per_device(
    residual,
    new_queries,
    new_keys,
    new_values,
    cache_keys,
    cache_values,
    lengths,
    out_weight,
    temporal_gain,
    in_weight,
    tokens,
    level_tables,
    depth_gain,
    depth_qkv,
    depth_out,
):
    shape = jax.ShapeDtypeStruct
    bf16, f32 = jnp.bfloat16, jnp.float32
    held, _, features = residual.shape
    tensor_size = lax.axis_size("tensor")
    batch_size = lax.axis_size("batch")
    rows = held * FRAMES
    width = in_weight.shape[1]
    members = batch_size // CORES
    count = FRAMES * LEVELS
    backward = [list(range(tensor_size))[::-1]]

    order = call(
        warm_kernel, "warm", pltpu.VMEM((8, 128), f32), [], VMEM, [], LIMIT, WARM_FLOPS, 1
    )()
    other_tables = lax.ppermute(level_tables, "batch", flipped(batch_size, 1, 1))
    near = [lax.ppermute(tokens, "batch", flipped(batch_size, CORES, s)) for s in STEPS]
    head_terms = call(
        attend_kernel,
        "attend",
        pltpu.HBM((tensor_size, rows, features), bf16),
        [ANY] + [VMEM] * 7,
        ANY,
        [
            pltpu.SMEM((held,), jnp.int32),
            pltpu.VMEM((3, rows, new_queries.shape[2]), f32),
            pltpu.VMEM((tensor_size, rows, features), bf16),
            pltpu.SemaphoreType.DMA((3 + tensor_size,)),
        ],
        LIMIT,
        10**8,
        4 * 2**20,
    )(
        *hbm(lengths),
        new_queries,
        new_keys,
        new_values,
        cache_keys,
        cache_values,
        out_weight,
        order,
    )
    column = call(
        gather_kernel,
        "gather",
        pltpu.VMEM((SIDE, FRAMES, LEVELS), jnp.int32),
        [VMEM] * SIDE + [ANY],
        VMEM,
        [],
        LIMIT,
        GATHER_FLOPS,
        1,
    )(tokens, *sorted_steps(near), head_terms)
    ids = [lax.ppermute(column, "batch", flipped(batch_size, CORES * SIDE, s)) for s in STEPS]

    shares = lax.all_to_all(
        head_terms, "tensor", 0, 0, axis_index_groups=backward, tiled=True
    )

    partial_rows = call(
        lookup_kernel,
        "lookup",
        [pltpu.VMEM((SIDE, count, width), bf16)] * SIDE,
        [VMEM] * (SIDE + 2),
        [VMEM] * SIDE,
        [
            pltpu.VMEM((members, count, width), bf16),
        ],
        LIMIT,
        10**11,
        1,
    )(column, *sorted_steps(ids), level_tables, other_tables)
    looked = call(
        warm_kernel, "warm_in", pltpu.VMEM((8, 128), f32), [VMEM], VMEM, [], LIMIT, WARM_FLOPS, 1
    )(partial_rows[0])
    *partial_rows, looked = lax.optimization_barrier((*partial_rows, looked))
    across = [
        lax.ppermute(partial_rows[s], "batch", flipped(batch_size, CORES * SIDE, s))
        for s in STEPS
    ]
    own_rows, *side_rows = call(
        collect_kernel,
        "collect",
        [pltpu.VMEM((count, width), bf16)] * SIDE,
        [VMEM] * SIDE,
        [VMEM] * SIDE,
        [],
        LIMIT,
        10**6,
        1,
    )(partial_rows[0], *across)
    along = [
        lax.ppermute(side_rows[s - 1], "batch", flipped(batch_size, CORES, s)) for s in STEPS
    ]

    temporal_out, sent = call(
        middle_kernel,
        "middle",
        (pltpu.HBM(residual.shape, bf16), pltpu.HBM((held, FRAMES, width + EXTRA), f32)),
        [VMEM] * 5,
        (VMEM, VMEM),
        [
            pltpu.VMEM((rows, features), f32),
            pltpu.VMEM((rows, width + EXTRA), f32),
        ],
        LIMIT,
        10**9,
        1,
    )(shares, residual, temporal_gain.astype(f32).reshape(1, features), in_weight, looked)
    terms = lax.all_to_all(
        sent, "tensor", 0, 0, axis_index_groups=backward, tiled=True
    )

    near_weights = call(
        fetch_kernel,
        "fetch",
        pltpu.VMEM(depth_qkv.shape, bf16),
        [ANY, ANY, VMEM],
        VMEM,
        [pltpu.SemaphoreType.DMA((1 + width // LATE,))],
        LIMIT,
        10**9,
        1,
    )(*hbm(depth_qkv, depth_out), own_rows)
    states = call(
        depth_kernel,
        "depth",
        pltpu.HBM((count, width), bf16),
        [VMEM] * (SIDE + 3) + [ANY, ANY],
        VMEM,
        [
            pltpu.VMEM((width, LATE), bf16),
            pltpu.VMEM((depth_out.shape[0] - LATE, width), bf16),
            pltpu.SemaphoreType.DMA((2,)),
        ],
        LIMIT,
        10**9,
        1,
    )(terms, own_rows, *along, depth_gain.astype(f32).reshape(1, width), near_weights, *hbm(depth_qkv, depth_out))
    return (temporal_out, states.reshape(1, FRAMES, LEVELS, width))


def solution(mesh):
    placed = (
        P("batch", None, "tensor"),
        P("batch", None, "tensor"),
        P("batch", None, "tensor"),
        P("batch", None, "tensor"),
        P("batch", None, "tensor"),
        P("batch", None, "tensor"),
        P("batch"),
        P("tensor", None),
        P("tensor"),
        P("tensor", None),
        P(("batch", "tensor"), None, None),
        P(None, "batch", None),
        P(),
        P(),
        P(),
    )
    return jax.shard_map(
        per_device,
        mesh=mesh,
        in_specs=placed,
        out_specs=(P("batch", None, "tensor"), P(("batch", "tensor"), None, None, None)),
        check_vma=False,
    )
```

```python
import functools
import math

import jax
import jax.numpy as jnp
from jax import lax
from jax.experimental import pallas as pl
from jax.experimental.pallas import tpu as pltpu
from jax.sharding import PartitionSpec as P

D = 4096
HD = 128
DD = 1024
DHD = 64
DHEADS = 8
LEVELS = 8
FRAMES = 2
CORES = 2
SIDE = 4
STEPS = (2, 1, 3)
LATE = 128
EXTRA = 128
MIB = 2**20
LIMIT = 16
WARM_FLOPS = 10**10
GATHER_FLOPS = 10**10
NT = (((1,), (1,)), ((), ()))


def dot_nt(a, b):
    return lax.dot_general(a, b, NT, preferred_element_type=jnp.float32)


def dot_nn(a, b):
    return jnp.dot(a, b, preferred_element_type=jnp.float32)


def iota(shape, axis):
    return lax.broadcasted_iota(jnp.int32, shape, axis)


def warm_kernel(*refs):
    refs[-1][...] = jnp.zeros_like(refs[-1])


def attend_kernel(
    lengths_ref, q_ref, nk_ref, nv_ref, k_ref, v_ref, w_ref, order_ref, out_hbm, small, sent_buf, sems
):
    dialogues = q_ref.shape[0]
    width = q_ref.shape[2]
    rows = dialogues * FRAMES
    heads = width // HD
    stacked = heads * rows
    slots = k_ref.shape[1]
    for i, ref in enumerate((q_ref, nk_ref, nv_ref)):
        for d in range(dialogues):
            small[i, FRAMES * d : FRAMES * (d + 1), :] = ref[d].astype(jnp.float32)
    query = small[0]
    fresh_key = small[1].astype(jnp.bfloat16)
    fresh_value = small[2].astype(jnp.bfloat16)
    head_of = iota((rows, width), 1) // HD
    spread = jnp.concatenate(
        [jnp.where(head_of == h, query, 0.0) for h in range(heads)], axis=0
    ).astype(jnp.bfloat16)
    scale = 1.0 / math.sqrt(HD)

    slot = iota((stacked, slots), 1)
    dialogue = (iota((stacked, slots), 0) % rows) // FRAMES
    of_dialogue = [dialogue == d for d in range(dialogues)]
    scores = jnp.zeros((stacked, slots), jnp.float32)
    for d in range(dialogues):
        scores = jnp.where(of_dialogue[d], dot_nt(spread, k_ref[d]), scores)
    row_n = iota((stacked, rows), 0) % rows
    col_n = iota((stacked, rows), 1)
    seen = (row_n // FRAMES == col_n // FRAMES) & (col_n <= row_n)
    fresh = jnp.where(seen, dot_nt(spread, fresh_key) * scale, -jnp.inf)
    row_d = (iota((stacked, dialogues), 0) % rows) // FRAMES
    live = jnp.sum(
        jnp.where(row_d == iota((stacked, dialogues), 1), lengths_ref[...].astype(jnp.float32), 0.0),
        axis=-1,
        keepdims=True,
    ).astype(jnp.int32)
    scores = jnp.where(slot < live, scores * scale, -jnp.inf)
    largest = jnp.maximum(
        jnp.max(scores, axis=-1, keepdims=True), jnp.max(fresh, axis=-1, keepdims=True)
    )
    exp_cache = jnp.exp(scores - largest)
    exp_fresh = jnp.exp(fresh - largest)
    total = jnp.sum(exp_cache, axis=-1, keepdims=True) + jnp.sum(
        exp_fresh, axis=-1, keepdims=True
    )
    mixed = dot_nn(exp_fresh.astype(jnp.bfloat16), fresh_value)
    for d in range(dialogues):
        own = jnp.where(of_dialogue[d], exp_cache, 0.0).astype(jnp.bfloat16)
        mixed = mixed + dot_nn(own, v_ref[d])
    mixed = mixed / total
    attended = mixed[:rows]
    for h in range(1, heads):
        attended = jnp.where(head_of == h, mixed[h * rows : (h + 1) * rows], attended)
    attended = attended.astype(jnp.bfloat16)
    peers, _, features = sent_buf.shape
    sends = []
    for t in range(peers):
        sent_buf[t] = dot_nn(attended, w_ref[:, t * features : (t + 1) * features]).astype(
            jnp.bfloat16
        )
        sends.append(pltpu.make_async_copy(sent_buf.at[t], out_hbm.at[peers - 1 - t], sems.at[3 + t]))
        sends[t].start()
    for send in sends:
        send.wait()


def gather_kernel(*refs):
    out_ref = refs[-1]
    for i in range(SIDE):
        out_ref[i] = refs[i][0]


def lookup_kernel(*refs):
    ids_refs, (own_ref, other_ref) = refs[:SIDE], refs[SIDE : SIDE + 2]
    out_refs, found_buf = refs[SIDE + 2 : 2 * SIDE + 2], refs[-1]
    span = own_ref.shape[1]
    width = own_ref.shape[2]
    entries = LEVELS * span
    count = FRAMES * LEVELS
    members = SIDE * SIDE
    rows = members * count
    me = lax.axis_index("batch")

    pick = (iota((rows, members), 0) // count == iota((rows, members), 1)).astype(jnp.bfloat16)
    row = iota((rows, LEVELS), 0)
    lane = iota((rows, LEVELS), 1)
    block = jnp.zeros((rows, LEVELS), jnp.float32)
    inner = jnp.zeros((rows, LEVELS), jnp.float32)
    for f in range(FRAMES):
        ids = jnp.concatenate([ref[:, f, :] for ref in ids_refs], axis=0)
        mine = (lane == row % LEVELS) & ((row // LEVELS) % FRAMES == f)
        high = (ids // span).astype(jnp.float32).astype(jnp.bfloat16)
        low = (ids % span).astype(jnp.float32).astype(jnp.bfloat16)
        block = jnp.where(mine, dot_nn(pick, high), block)
        inner = jnp.where(mine, dot_nn(pick, low), inner)
    block = jnp.sum(block, axis=1, keepdims=True).astype(jnp.int32)
    inner = jnp.sum(inner, axis=1, keepdims=True).astype(jnp.int32)
    level = iota((rows, 1), 0) % LEVELS
    place = inner + level * span
    at_own = jnp.where(block == me, place, -1)
    at_other = jnp.where(block == (me ^ 1), place, -1)
    entry = iota((rows, entries), 1)
    hot_own = jnp.where(entry == at_own, 1.0, 0.0).astype(jnp.bfloat16)
    hot_other = jnp.where(entry == at_other, 1.0, 0.0).astype(jnp.bfloat16)
    found = dot_nn(hot_own, own_ref[...].reshape(entries, width))
    found = found + dot_nn(hot_other, other_ref[...].reshape(entries, width))
    found_buf[...] = found.astype(jnp.bfloat16).reshape(found_buf.shape)
    for s in range(SIDE):
        out_refs[s][...] = found_buf[s * SIDE : (s + 1) * SIDE]


def collect_kernel(own_ref, *refs):
    arrived, out_refs = refs[: SIDE - 1], refs[SIDE - 1 :]
    for s in range(SIDE):
        value = own_ref[s]
        for ref in arrived:
            value = value + ref[s]
        out_refs[s][...] = value


def fetch_kernel(qkv_hbm, o_hbm, order_ref, out_ref, sems):
    near = qkv_hbm.shape[1] - LATE
    copies = [
        pltpu.make_async_copy(qkv_hbm.at[:, pl.ds(0, near)], out_ref.at[:, pl.ds(0, near)], sems.at[0])
    ]
    for j in range(o_hbm.shape[1] // LATE):
        part = pl.ds(j * LATE, LATE)
        copies.append(
            pltpu.make_async_copy(
                o_hbm.at[pl.ds(0, LATE), part], out_ref.at[part, pl.ds(near, LATE)], sems.at[1 + j]
            )
        )
    for copy in copies:
        copy.start()
    for copy in copies:
        copy.wait()


def middle_kernel(
    shares_ref, residual_ref, gain_ref, w_ref, order_ref, stream_ref, sent_ref, rows_buf, sent_buf
):
    dialogues = residual_ref.shape[0]
    for d in range(dialogues):
        rows_buf[FRAMES * d : FRAMES * (d + 1), :] = residual_ref[d].astype(jnp.float32)
    hidden = rows_buf[...]
    share = shares_ref[0].astype(jnp.float32)
    for t in range(1, shares_ref.shape[0]):
        share = share + shares_ref[t].astype(jnp.float32)
    hidden = hidden + share
    rows_buf[...] = hidden
    squares = jnp.sum(hidden * hidden, axis=-1, keepdims=True)
    scaled = (hidden * gain_ref[...]).astype(jnp.bfloat16)
    width = w_ref.shape[1]
    sent_buf[:, width:] = jnp.broadcast_to(squares, (hidden.shape[0], EXTRA))
    for d in range(dialogues):
        stream_ref[d] = rows_buf[FRAMES * d : FRAMES * (d + 1), :].astype(jnp.bfloat16)
    sent_buf[:, :width] = dot_nn(scaled, w_ref[...])
    for d in range(dialogues):
        sent_ref[dialogues - 1 - d] = sent_buf[FRAMES * d : FRAMES * (d + 1), :]


def depth_kernel(
    terms_ref, *refs
):
    table_refs = refs[:SIDE]
    gain_ref, near_ref, qkv_hbm, o_hbm, out_ref, v_buf, o_buf, sems = refs[SIDE:]
    heads_width = DHEADS * DHD
    near = 3 * heads_width - LATE
    get_v = pltpu.make_async_copy(qkv_hbm.at[:, pl.ds(near, LATE)], v_buf, sems.at[0])
    get_o = pltpu.make_async_copy(
        o_hbm.at[pl.ds(LATE, heads_width - LATE)], o_buf, sems.at[1]
    )
    get_v.start()
    get_o.start()
    count, width = table_refs[0].shape
    terms = terms_ref[0]
    for t in range(1, terms_ref.shape[0]):
        terms = terms + terms_ref[t]
    inverse = lax.rsqrt(terms[:, width : width + 1] / D + 1e-05)
    proj = terms[:, :width] * inverse
    values = table_refs[0][...].astype(jnp.float32)
    for ref in table_refs[1:]:
        values = values + ref[...].astype(jnp.float32)
    frame = iota((count, width), 0) // LEVELS
    depth_input = values + jnp.where(frame == 0, proj[0:1], proj[1:2])
    mean = jnp.sum(depth_input * depth_input, axis=-1, keepdims=True) / width
    normed = (depth_input * lax.rsqrt(mean + 1e-05) * gain_ref[...]).astype(jnp.bfloat16)
    query = dot_nn(normed, near_ref[:, :heads_width]).astype(jnp.bfloat16).astype(jnp.float32)
    key = dot_nn(normed, near_ref[:, heads_width : 2 * heads_width]).astype(jnp.bfloat16)
    value = dot_nn(normed, near_ref[:, 2 * heads_width : near]).astype(jnp.bfloat16)
    head_of = iota((count, heads_width), 1) // DHD
    spread = jnp.concatenate(
        [jnp.where(head_of == h, query, 0.0) for h in range(DHEADS)], axis=0
    ).astype(jnp.bfloat16)
    scores = dot_nt(spread, key) * (1.0 / math.sqrt(DHD))
    row = iota(scores.shape, 0) % count
    col = iota(scores.shape, 1)
    seen = (row // LEVELS == col // LEVELS) & (col <= row)
    exps = jnp.where(seen, jnp.exp(scores), 0.0)
    probs = (exps / jnp.sum(exps, axis=-1, keepdims=True)).astype(jnp.bfloat16)
    get_v.wait()
    late_value = dot_nn(normed, v_buf[...]).astype(jnp.bfloat16)
    spread_out = dot_nn(probs, jnp.concatenate([value, late_value], axis=1))
    mixed = spread_out[:count]
    for h in range(1, DHEADS):
        mixed = jnp.where(head_of == h, spread_out[h * count : (h + 1) * count], mixed)
    mixed = mixed.astype(jnp.bfloat16)
    early = jnp.concatenate(
        [
            dot_nn(mixed[:, :LATE], near_ref[j * LATE : (j + 1) * LATE, near:])
            for j in range(width // LATE)
        ],
        axis=1,
    )
    get_o.wait()
    late = dot_nn(mixed[:, LATE:], o_buf[...])
    out_ref[...] = (depth_input + early + late).astype(jnp.bfloat16)


VMEM = pl.BlockSpec(memory_space=pltpu.VMEM)
SMEM = pl.BlockSpec(memory_space=pltpu.SMEM)
ANY = pl.BlockSpec(memory_space=pl.ANY)


def hbm(*arrays):
    return tuple(pltpu.with_memory_space_constraint(a, pltpu.HBM) for a in arrays)


def call(kernel, name, outs, ins, out_specs, scratch, limit, flops, moved):
    return pl.pallas_call(
        kernel,
        name=name,
        out_shape=outs,
        in_specs=ins,
        out_specs=out_specs,
        scratch_shapes=scratch,
        compiler_params=pltpu.CompilerParams(vmem_limit_bytes=limit * MIB),
        cost_estimate=pl.CostEstimate(flops=flops, bytes_accessed=moved, transcendentals=0),
    )


def flipped(size, step, s):
    span = SIDE * step
    return [(b, b // span * span + (b % span // step ^ s) * step + b % step) for b in range(size)]


def sorted_steps(arrays):
    return [arrays[STEPS.index(s)] for s in range(1, SIDE)]


def per_device(
    residual,
    new_queries,
    new_keys,
    new_values,
    cache_keys,
    cache_values,
    lengths,
    out_weight,
    temporal_gain,
    in_weight,
    tokens,
    level_tables,
    depth_gain,
    depth_qkv,
    depth_out,
):
    shape = jax.ShapeDtypeStruct
    bf16, f32 = jnp.bfloat16, jnp.float32
    held, _, features = residual.shape
    tensor_size = lax.axis_size("tensor")
    batch_size = lax.axis_size("batch")
    rows = held * FRAMES
    width = in_weight.shape[1]
    members = batch_size // CORES
    count = FRAMES * LEVELS
    backward = [list(range(tensor_size))[::-1]]

    order = call(
        warm_kernel, "warm", pltpu.VMEM((8, 128), f32), [], VMEM, [], LIMIT, WARM_FLOPS, 1
    )()
    other_tables = lax.ppermute(level_tables, "batch", flipped(batch_size, 1, 1))
    near = [lax.ppermute(tokens, "batch", flipped(batch_size, CORES, s)) for s in STEPS]
    head_terms = call(
        attend_kernel,
        "attend",
        pltpu.HBM((tensor_size, rows, features), bf16),
        [VMEM] * 8,
        ANY,
        [
            pltpu.VMEM((3, rows, new_queries.shape[2]), f32),
            pltpu.VMEM((tensor_size, rows, features), bf16),
            pltpu.SemaphoreType.DMA((3 + tensor_size,)),
        ],
        LIMIT,
        10**8,
        4 * 2**20,
    )(
        lengths.reshape(1, held),
        new_queries,
        new_keys,
        new_values,
        cache_keys,
        cache_values,
        out_weight,
        order,
    )
    column = call(
        gather_kernel,
        "gather",
        pltpu.VMEM((SIDE, FRAMES, LEVELS), jnp.int32),
        [VMEM] * SIDE + [ANY],
        VMEM,
        [],
        LIMIT,
        GATHER_FLOPS,
        1,
    )(tokens, *sorted_steps(near), head_terms)
    ids = [lax.ppermute(column, "batch", flipped(batch_size, CORES * SIDE, s)) for s in STEPS]

    shares = lax.all_to_all(
        head_terms, "tensor", 0, 0, axis_index_groups=backward, tiled=True
    )

    partial_rows = call(
        lookup_kernel,
        "lookup",
        [pltpu.VMEM((SIDE, count, width), bf16)] * SIDE,
        [VMEM] * (SIDE + 2),
        [VMEM] * SIDE,
        [
            pltpu.VMEM((members, count, width), bf16),
        ],
        LIMIT,
        10**11,
        1,
    )(column, *sorted_steps(ids), level_tables, other_tables)
    looked = call(
        warm_kernel, "warm_in", pltpu.VMEM((8, 128), f32), [VMEM], VMEM, [], LIMIT, WARM_FLOPS, 1
    )(partial_rows[0])
    *partial_rows, looked = lax.optimization_barrier((*partial_rows, looked))
    across = [
        lax.ppermute(partial_rows[s], "batch", flipped(batch_size, CORES * SIDE, s))
        for s in STEPS
    ]
    own_rows, *side_rows = call(
        collect_kernel,
        "collect",
        [pltpu.VMEM((count, width), bf16)] * SIDE,
        [VMEM] * SIDE,
        [VMEM] * SIDE,
        [],
        LIMIT,
        10**6,
        1,
    )(partial_rows[0], *across)
    along = [
        lax.ppermute(side_rows[s - 1], "batch", flipped(batch_size, CORES, s)) for s in STEPS
    ]

    temporal_out, sent = call(
        middle_kernel,
        "middle",
        (pltpu.HBM(residual.shape, bf16), pltpu.HBM((held, FRAMES, width + EXTRA), f32)),
        [VMEM] * 5,
        (VMEM, VMEM),
        [
            pltpu.VMEM((rows, features), f32),
            pltpu.VMEM((rows, width + EXTRA), f32),
        ],
        LIMIT,
        10**9,
        1,
    )(shares, residual, temporal_gain.astype(f32).reshape(1, features), in_weight, looked)
    terms = lax.all_to_all(
        sent, "tensor", 0, 0, axis_index_groups=backward, tiled=True
    )

    near_weights = call(
        fetch_kernel,
        "fetch",
        pltpu.VMEM(depth_qkv.shape, bf16),
        [ANY, ANY, VMEM],
        VMEM,
        [pltpu.SemaphoreType.DMA((1 + width // LATE,))],
        LIMIT,
        10**9,
        1,
    )(*hbm(depth_qkv, depth_out), own_rows)
    states = call(
        depth_kernel,
        "depth",
        pltpu.HBM((count, width), bf16),
        [VMEM] * (SIDE + 3) + [ANY, ANY],
        VMEM,
        [
            pltpu.VMEM((width, LATE), bf16),
            pltpu.VMEM((depth_out.shape[0] - LATE, width), bf16),
            pltpu.SemaphoreType.DMA((2,)),
        ],
        LIMIT,
        10**9,
        1,
    )(terms, own_rows, *along, depth_gain.astype(f32).reshape(1, width), near_weights, *hbm(depth_qkv, depth_out))
    return (temporal_out, states.reshape(1, FRAMES, LEVELS, width))


def solution(mesh):
    placed = (
        P("batch", None, "tensor"),
        P("batch", None, "tensor"),
        P("batch", None, "tensor"),
        P("batch", None, "tensor"),
        P("batch", None, "tensor"),
        P("batch", None, "tensor"),
        P("batch"),
        P("tensor", None),
        P("tensor"),
        P("tensor", None),
        P(("batch", "tensor"), None, None),
        P(None, "batch", None),
        P(),
        P(),
        P(),
    )
    return jax.shard_map(
        per_device,
        mesh=mesh,
        in_specs=placed,
        out_specs=(P("batch", None, "tensor"), P(("batch", "tensor"), None, None, None)),
        check_vma=False,
    )
```

```python
import functools
import math

import jax
import jax.numpy as jnp
from jax import lax
from jax.experimental import pallas as pl
from jax.experimental.pallas import tpu as pltpu
from jax.sharding import PartitionSpec as P

D = 4096
HD = 128
DD = 1024
DHD = 64
DHEADS = 8
LEVELS = 8
FRAMES = 2
CORES = 2
SIDE = 4
STEPS = (2, 1, 3)
LATE = 128
EXTRA = 128
MIB = 2**20
LIMIT = 16
WARM_FLOPS = 10**10
GATHER_FLOPS = 10**10
NT = (((1,), (1,)), ((), ()))


def dot_nt(a, b):
    return lax.dot_general(a, b, NT, preferred_element_type=jnp.float32)


def dot_nn(a, b):
    return jnp.dot(a, b, preferred_element_type=jnp.float32)


def iota(shape, axis):
    return lax.broadcasted_iota(jnp.int32, shape, axis)


def warm_kernel(*refs):
    refs[-1][...] = jnp.zeros_like(refs[-1])


def attend_kernel(
    lengths_ref, q_ref, nk_ref, nv_ref, k_ref, v_ref, w_ref, order_ref, out_hbm, small, sent_buf, sems
):
    dialogues = q_ref.shape[0]
    width = q_ref.shape[2]
    rows = dialogues * FRAMES
    heads = width // HD
    stacked = heads * rows
    slots = k_ref.shape[1]
    for i, ref in enumerate((q_ref, nk_ref, nv_ref)):
        for d in range(dialogues):
            small[i, FRAMES * d : FRAMES * (d + 1), :] = ref[d].astype(jnp.float32)
    query = small[0]
    fresh_key = small[1].astype(jnp.bfloat16)
    fresh_value = small[2].astype(jnp.bfloat16)
    head_of = iota((rows, width), 1) // HD
    spread = jnp.concatenate(
        [jnp.where(head_of == h, query, 0.0) for h in range(heads)], axis=0
    ).astype(jnp.bfloat16)
    scale = 1.0 / math.sqrt(HD)

    slot = iota((stacked, slots), 1)
    dialogue = (iota((stacked, slots), 0) % rows) // FRAMES
    of_dialogue = [dialogue == d for d in range(dialogues)]
    scores = jnp.zeros((stacked, slots), jnp.float32)
    for d in range(dialogues):
        scores = jnp.where(of_dialogue[d], dot_nt(spread, k_ref[d]), scores)
    row_n = iota((stacked, rows), 0) % rows
    col_n = iota((stacked, rows), 1)
    seen = (row_n // FRAMES == col_n // FRAMES) & (col_n <= row_n)
    fresh = jnp.where(seen, dot_nt(spread, fresh_key) * scale, -jnp.inf)
    row_d = (iota((stacked, dialogues), 0) % rows) // FRAMES
    live = jnp.sum(
        jnp.where(row_d == iota((stacked, dialogues), 1), lengths_ref[...].astype(jnp.float32), 0.0),
        axis=-1,
        keepdims=True,
    ).astype(jnp.int32)
    scores = jnp.where(slot < live, scores * scale, -jnp.inf)
    largest = jnp.maximum(
        jnp.max(scores, axis=-1, keepdims=True), jnp.max(fresh, axis=-1, keepdims=True)
    )
    exp_cache = jnp.exp(scores - largest)
    exp_fresh = jnp.exp(fresh - largest)
    total = jnp.sum(exp_cache, axis=-1, keepdims=True) + jnp.sum(
        exp_fresh, axis=-1, keepdims=True
    )
    mixed = dot_nn(exp_fresh.astype(jnp.bfloat16), fresh_value)
    for d in range(dialogues):
        own = jnp.where(of_dialogue[d], exp_cache, 0.0).astype(jnp.bfloat16)
        mixed = mixed + dot_nn(own, v_ref[d])
    mixed = mixed / total
    attended = mixed[:rows]
    for h in range(1, heads):
        attended = jnp.where(head_of == h, mixed[h * rows : (h + 1) * rows], attended)
    attended = attended.astype(jnp.bfloat16)
    peers, _, features = sent_buf.shape
    sends = []
    for t in range(peers):
        sent_buf[t] = dot_nn(attended, w_ref[:, t * features : (t + 1) * features]).astype(
            jnp.bfloat16
        )
        sends.append(pltpu.make_async_copy(sent_buf.at[t], out_hbm.at[peers - 1 - t], sems.at[3 + t]))
        sends[t].start()
    for send in sends:
        send.wait()


def gather_kernel(*refs):
    out_ref = refs[-1]
    for i in range(SIDE):
        out_ref[i] = refs[i][0]


def lookup_kernel(*refs):
    ids_refs, (own_ref, other_ref) = refs[:SIDE], refs[SIDE : SIDE + 2]
    out_refs, found_buf = refs[SIDE + 2 : 2 * SIDE + 2], refs[-1]
    span = own_ref.shape[1]
    width = own_ref.shape[2]
    entries = LEVELS * span
    count = FRAMES * LEVELS
    members = SIDE * SIDE
    rows = members * count
    me = lax.axis_index("batch")

    pick = (iota((rows, members), 0) // count == iota((rows, members), 1)).astype(jnp.bfloat16)
    row = iota((rows, LEVELS), 0)
    lane = iota((rows, LEVELS), 1)
    block = jnp.zeros((rows, LEVELS), jnp.float32)
    inner = jnp.zeros((rows, LEVELS), jnp.float32)
    for f in range(FRAMES):
        ids = jnp.concatenate([ref[:, f, :] for ref in ids_refs], axis=0)
        mine = (lane == row % LEVELS) & ((row // LEVELS) % FRAMES == f)
        high = (ids // span).astype(jnp.float32).astype(jnp.bfloat16)
        low = (ids % span).astype(jnp.float32).astype(jnp.bfloat16)
        block = jnp.where(mine, dot_nn(pick, high), block)
        inner = jnp.where(mine, dot_nn(pick, low), inner)
    block = jnp.sum(block, axis=1, keepdims=True).astype(jnp.int32)
    inner = jnp.sum(inner, axis=1, keepdims=True).astype(jnp.int32)
    level = iota((rows, 1), 0) % LEVELS
    place = inner + level * span
    at_own = jnp.where(block == me, place, -1)
    at_other = jnp.where(block == (me ^ 1), place, -1)
    entry = iota((rows, entries), 1)
    hot_own = jnp.where(entry == at_own, 1.0, 0.0).astype(jnp.bfloat16)
    hot_other = jnp.where(entry == at_other, 1.0, 0.0).astype(jnp.bfloat16)
    found = dot_nn(hot_own, own_ref[...].reshape(entries, width))
    found = found + dot_nn(hot_other, other_ref[...].reshape(entries, width))
    found_buf[...] = found.astype(jnp.bfloat16).reshape(found_buf.shape)
    for s in range(SIDE):
        out_refs[s][...] = found_buf[s * SIDE : (s + 1) * SIDE]


def collect_kernel(own_ref, *refs):
    arrived, out_refs = refs[: SIDE - 1], refs[SIDE - 1 :]
    for s in range(SIDE):
        value = own_ref[s]
        for ref in arrived:
            value = value + ref[s]
        out_refs[s][...] = value


def fetch_kernel(qkv_hbm, o_hbm, order_ref, out_ref, sems):
    near = qkv_hbm.shape[1] - LATE
    copies = [
        pltpu.make_async_copy(qkv_hbm.at[:, pl.ds(0, near)], out_ref.at[:, pl.ds(0, near)], sems.at[0])
    ]
    for j in range(o_hbm.shape[1] // LATE):
        part = pl.ds(j * LATE, LATE)
        copies.append(
            pltpu.make_async_copy(
                o_hbm.at[pl.ds(0, LATE), part], out_ref.at[part, pl.ds(near, LATE)], sems.at[1 + j]
            )
        )
    for copy in copies:
        copy.start()
    for copy in copies:
        copy.wait()


def middle_kernel(
    shares_ref, residual_ref, gain_ref, w_ref, order_ref, stream_ref, sent_ref, rows_buf, sent_buf
):
    dialogues = residual_ref.shape[0]
    for d in range(dialogues):
        rows_buf[FRAMES * d : FRAMES * (d + 1), :] = residual_ref[d].astype(jnp.float32)
    hidden = rows_buf[...]
    share = shares_ref[0].astype(jnp.float32)
    for t in range(1, shares_ref.shape[0]):
        share = share + shares_ref[t].astype(jnp.float32)
    hidden = hidden + share
    rows_buf[...] = hidden
    squares = jnp.sum(hidden * hidden, axis=-1, keepdims=True)
    scaled = (hidden * gain_ref[...]).astype(jnp.bfloat16)
    width = w_ref.shape[1]
    sent_buf[:, width:] = jnp.broadcast_to(squares, (hidden.shape[0], EXTRA))
    for d in range(dialogues):
        stream_ref[d] = rows_buf[FRAMES * d : FRAMES * (d + 1), :].astype(jnp.bfloat16)
    sent_buf[:, :width] = dot_nn(scaled, w_ref[...])
    for d in range(dialogues):
        sent_ref[dialogues - 1 - d] = sent_buf[FRAMES * d : FRAMES * (d + 1), :]


def depth_kernel(
    terms_ref, *refs
):
    table_refs = refs[:SIDE]
    gain_ref, near_ref, qkv_hbm, o_hbm, out_ref, v_buf, o_buf, sems = refs[SIDE:]
    heads_width = DHEADS * DHD
    near = 3 * heads_width - LATE
    get_v = pltpu.make_async_copy(qkv_hbm.at[:, pl.ds(near, LATE)], v_buf, sems.at[0])
    get_o = pltpu.make_async_copy(
        o_hbm.at[pl.ds(LATE, heads_width - LATE)], o_buf, sems.at[1]
    )
    get_v.start()
    get_o.start()
    count, width = table_refs[0].shape
    terms = terms_ref[0]
    for t in range(1, terms_ref.shape[0]):
        terms = terms + terms_ref[t]
    inverse = lax.rsqrt(terms[:, width : width + 1] / D + 1e-05)
    proj = terms[:, :width] * inverse
    values = table_refs[0][...].astype(jnp.float32)
    for ref in table_refs[1:]:
        values = values + ref[...].astype(jnp.float32)
    frame = iota((count, width), 0) // LEVELS
    depth_input = values + jnp.where(frame == 0, proj[0:1], proj[1:2])
    mean = jnp.sum(depth_input * depth_input, axis=-1, keepdims=True) / width
    normed = (depth_input * lax.rsqrt(mean + 1e-05) * gain_ref[...]).astype(jnp.bfloat16)
    query = dot_nn(normed, near_ref[:, :heads_width]).astype(jnp.bfloat16).astype(jnp.float32)
    key = dot_nn(normed, near_ref[:, heads_width : 2 * heads_width]).astype(jnp.bfloat16)
    value = dot_nn(normed, near_ref[:, 2 * heads_width : near]).astype(jnp.bfloat16)
    head_of = iota((count, heads_width), 1) // DHD
    spread = jnp.concatenate(
        [jnp.where(head_of == h, query, 0.0) for h in range(DHEADS)], axis=0
    ).astype(jnp.bfloat16)
    scores = dot_nt(spread, key) * (1.0 / math.sqrt(DHD))
    row = iota(scores.shape, 0) % count
    col = iota(scores.shape, 1)
    seen = (row // LEVELS == col // LEVELS) & (col <= row)
    exps = jnp.where(seen, jnp.exp(scores), 0.0)
    probs = (exps / jnp.sum(exps, axis=-1, keepdims=True)).astype(jnp.bfloat16)
    get_v.wait()
    late_value = dot_nn(normed, v_buf[...]).astype(jnp.bfloat16)
    spread_out = dot_nn(probs, jnp.concatenate([value, late_value], axis=1))
    mixed = spread_out[:count]
    for h in range(1, DHEADS):
        mixed = jnp.where(head_of == h, spread_out[h * count : (h + 1) * count], mixed)
    mixed = mixed.astype(jnp.bfloat16)
    early = jnp.concatenate(
        [
            dot_nn(mixed[:, :LATE], near_ref[j * LATE : (j + 1) * LATE, near:])
            for j in range(width // LATE)
        ],
        axis=1,
    )
    get_o.wait()
    late = dot_nn(mixed[:, LATE:], o_buf[...])
    out_ref[...] = (depth_input + early + late).astype(jnp.bfloat16)


VMEM = pl.BlockSpec(memory_space=pltpu.VMEM)
SMEM = pl.BlockSpec(memory_space=pltpu.SMEM)
ANY = pl.BlockSpec(memory_space=pl.ANY)


def hbm(*arrays):
    return tuple(pltpu.with_memory_space_constraint(a, pltpu.HBM) for a in arrays)


def call(kernel, name, outs, ins, out_specs, scratch, limit, flops, moved):
    return pl.pallas_call(
        kernel,
        name=name,
        out_shape=outs,
        in_specs=ins,
        out_specs=out_specs,
        scratch_shapes=scratch,
        compiler_params=pltpu.CompilerParams(vmem_limit_bytes=limit * MIB),
        cost_estimate=pl.CostEstimate(flops=flops, bytes_accessed=moved, transcendentals=0),
    )


def flipped(size, step, s):
    span = SIDE * step
    return [(b, b // span * span + (b % span // step ^ s) * step + b % step) for b in range(size)]


def sorted_steps(arrays):
    return [arrays[STEPS.index(s)] for s in range(1, SIDE)]


def per_device(
    residual,
    new_queries,
    new_keys,
    new_values,
    cache_keys,
    cache_values,
    lengths,
    out_weight,
    temporal_gain,
    in_weight,
    tokens,
    level_tables,
    depth_gain,
    depth_qkv,
    depth_out,
):
    shape = jax.ShapeDtypeStruct
    bf16, f32 = jnp.bfloat16, jnp.float32
    held, _, features = residual.shape
    tensor_size = lax.axis_size("tensor")
    batch_size = lax.axis_size("batch")
    rows = held * FRAMES
    width = in_weight.shape[1]
    members = batch_size // CORES
    count = FRAMES * LEVELS
    backward = [list(range(tensor_size))[::-1]]

    order = call(
        warm_kernel, "warm", pltpu.VMEM((8, 128), f32), [], VMEM, [], LIMIT, WARM_FLOPS, 1
    )()
    other_tables = lax.ppermute(level_tables, "batch", flipped(batch_size, 1, 1))
    near = [lax.ppermute(tokens, "batch", flipped(batch_size, CORES, s)) for s in range(1, SIDE)]
    head_terms = call(
        attend_kernel,
        "attend",
        pltpu.HBM((tensor_size, rows, features), bf16),
        [VMEM] * 8,
        ANY,
        [
            pltpu.VMEM((3, rows, new_queries.shape[2]), f32),
            pltpu.VMEM((tensor_size, rows, features), bf16),
            pltpu.SemaphoreType.DMA((3 + tensor_size,)),
        ],
        LIMIT,
        10**8,
        4 * 2**20,
    )(
        lengths.reshape(1, held),
        new_queries,
        new_keys,
        new_values,
        cache_keys,
        cache_values,
        out_weight,
        order,
    )
    column = call(
        gather_kernel,
        "gather",
        pltpu.VMEM((SIDE, FRAMES, LEVELS), jnp.int32),
        [VMEM] * SIDE + [ANY],
        VMEM,
        [],
        LIMIT,
        GATHER_FLOPS,
        1,
    )(tokens, *near, head_terms)
    ids = [lax.ppermute(column, "batch", flipped(batch_size, CORES * SIDE, s)) for s in STEPS]

    shares = lax.all_to_all(
        head_terms, "tensor", 0, 0, axis_index_groups=backward, tiled=True
    )

    partial_rows = call(
        lookup_kernel,
        "lookup",
        [pltpu.VMEM((SIDE, count, width), bf16)] * SIDE,
        [VMEM] * (SIDE + 2),
        [VMEM] * SIDE,
        [
            pltpu.VMEM((members, count, width), bf16),
        ],
        LIMIT,
        10**11,
        1,
    )(column, *sorted_steps(ids), level_tables, other_tables)
    looked = call(
        warm_kernel, "warm_in", pltpu.VMEM((8, 128), f32), [VMEM], VMEM, [], LIMIT, WARM_FLOPS, 1
    )(partial_rows[0])
    *partial_rows, looked = lax.optimization_barrier((*partial_rows, looked))
    across = [
        lax.ppermute(partial_rows[s], "batch", flipped(batch_size, CORES * SIDE, s))
        for s in STEPS
    ]
    own_rows, *side_rows = call(
        collect_kernel,
        "collect",
        [pltpu.VMEM((count, width), bf16)] * SIDE,
        [VMEM] * SIDE,
        [VMEM] * SIDE,
        [],
        LIMIT,
        10**6,
        1,
    )(partial_rows[0], *across)
    along = [
        lax.ppermute(side_rows[s - 1], "batch", flipped(batch_size, CORES, s)) for s in STEPS
    ]

    temporal_out, sent = call(
        middle_kernel,
        "middle",
        (pltpu.HBM(residual.shape, bf16), pltpu.HBM((held, FRAMES, width + EXTRA), f32)),
        [VMEM] * 5,
        (VMEM, VMEM),
        [
            pltpu.VMEM((rows, features), f32),
            pltpu.VMEM((rows, width + EXTRA), f32),
        ],
        LIMIT,
        10**9,
        1,
    )(shares, residual, temporal_gain.astype(f32).reshape(1, features), in_weight, looked)
    terms = lax.all_to_all(
        sent, "tensor", 0, 0, axis_index_groups=backward, tiled=True
    )

    near_weights = call(
        fetch_kernel,
        "fetch",
        pltpu.VMEM(depth_qkv.shape, bf16),
        [ANY, ANY, VMEM],
        VMEM,
        [pltpu.SemaphoreType.DMA((1 + width // LATE,))],
        LIMIT,
        10**9,
        1,
    )(*hbm(depth_qkv, depth_out), own_rows)
    states = call(
        depth_kernel,
        "depth",
        pltpu.HBM((count, width), bf16),
        [VMEM] * (SIDE + 3) + [ANY, ANY],
        VMEM,
        [
            pltpu.VMEM((width, LATE), bf16),
            pltpu.VMEM((depth_out.shape[0] - LATE, width), bf16),
            pltpu.SemaphoreType.DMA((2,)),
        ],
        LIMIT,
        10**9,
        1,
    )(terms, own_rows, *along, depth_gain.astype(f32).reshape(1, width), near_weights, *hbm(depth_qkv, depth_out))
    return (temporal_out, states.reshape(1, FRAMES, LEVELS, width))


def solution(mesh):
    placed = (
        P("batch", None, "tensor"),
        P("batch", None, "tensor"),
        P("batch", None, "tensor"),
        P("batch", None, "tensor"),
        P("batch", None, "tensor"),
        P("batch", None, "tensor"),
        P("batch"),
        P("tensor", None),
        P("tensor"),
        P("tensor", None),
        P(("batch", "tensor"), None, None),
        P(None, "batch", None),
        P(),
        P(),
        P(),
    )
    return jax.shard_map(
        per_device,
        mesh=mesh,
        in_specs=placed,
        out_specs=(P("batch", None, "tensor"), P(("batch", "tensor"), None, None, None)),
        check_vma=False,
    )
```
